512 devices in a mesh: dp: 16 (over z_lo, x), fsdp: 32 (over y, z_hi, core).
Axes of the slice: x: 4, y: 4, z: 16 (z_hi: 4, z_lo: 4; z = z_hi * 4 + z_lo), core: 2. Of those that a mesh axis runs over, the one named last changes fastest.
Arguments:
- normed_input: bfloat16 [65536, 8192], P(('dp', 'fsdp')), may hold values from -6 to 6
- value_cotangent: bfloat16 [65536, 1024], P(('dp', 'fsdp')), may hold values from -6 to 6
- basis: bfloat16 [8192, 512], P('fsdp'), may hold values from -0.25 to 0.25
- first_moment: float32 [512, 1024], P(('dp', 'fsdp')), may hold values from -6 to 6
- second_moment: float32 [512, 1024], P(('dp', 'fsdp')), may hold values from 1 to 30
Outputs:
- new_first_moment: float32 [512, 1024], P(('dp', 'fsdp'))
- new_second_moment: float32 [512, 1024], P(('dp', 'fsdp'))
- value_update: bfloat16 [8192, 1024], P('fsdp')
The draws below stay inside these ranges and needn't reach their ends.
All inputs are finite; a program needn't handle non-finite values.
Results may differ from the reference program's by a relative error of at most 0.0049.
The reference program's roundings to bfloat16 on the way (of `normalized`) count: a program that leaves them out, or rounds other values in their place, can miss the bound.
Values may be sent and summed in bfloat16 or wider, within the bound.
No kernel may reach another device: no remote copies, remote signals or barrier semaphores. Data moves between devices by JAX's collectives and lax.ppermute only.
A program may use at most 64 MiB of HBM per device.

```python
import math
import jax
import jax.numpy as jnp
from jax import lax

D = 8192
KVW = 1024
RANK = 512
STEP = 1000
TOKENS = 65536


def level_of(rng, shape, cuts, least, top_value):
    factor_of = 1.0
    for position, parts in cuts:
        heights = jax.random.uniform(jax.random.fold_in(jax.random.fold_in(rng, 6), position), (parts,), jnp.float32, least / len(cuts), top_value / len(cuts))
        factor_of = factor_of * jnp.repeat(jnp.exp(heights), shape[position] // parts).reshape((-1,) + (1,) * (len(shape) - 1 - position))
    return factor_of


def centred(rng, dims, deviation, most, cuts=(), kind=jnp.bfloat16):
    values = deviation * jax.random.normal(rng, dims, jnp.float32)
    if cuts:
        values = values * level_of(rng, dims, cuts, -0.22, 0.18)
    return jnp.clip(values, -most, most).astype(kind)


def setup_inputs(seed: int = 0) -> dict:
    arg_keys = jax.random.split(jax.random.key(seed), 6)
    return {
        "normed_input": centred(arg_keys[0], (TOKENS, D), 1.0, 6.0, ((0, 512),)),
        "value_cotangent": centred(arg_keys[1], (TOKENS, KVW), 1.0, 6.0, ((0, 512),)),
        "basis": centred(arg_keys[2], (D, RANK), RANK ** -0.5, 0.25, ((0, 32),)),
        "first_moment": centred(arg_keys[3], (RANK, KVW), 1.0, 6.0, ((0, 512),), jnp.float32),
        "second_moment": jnp.clip(jnp.exp(math.log(30.0) - 3.4011974 * jax.random.uniform(arg_keys[4], (RANK, KVW), jnp.float32) ** level_of(arg_keys[4], (RANK, KVW), ((0, 512),), -0.2, 0.2)), 1.0, 30.0),
    }


def reference(normed_input, value_cotangent, basis, first_moment, second_moment):
    reduced = jnp.dot(normed_input, basis, preferred_element_type=jnp.float32)
    projected = lax.dot_general(reduced, value_cotangent.astype(jnp.float32), (((0,), (0,)), ((), ())), precision=lax.Precision.HIGHEST)
    projected = projected / jnp.sqrt(jnp.float32(TOKENS))
    new_first = 0.9 * first_moment + 0.1 * projected
    new_second = 0.999 * second_moment + 0.001 * projected * projected
    corr_first = 1.0 - 0.9 ** STEP
    corr_second = 1.0 - 0.999 ** STEP
    normalized = (new_first / corr_first / (jnp.sqrt(new_second / corr_second) + 1e-08)).astype(jnp.bfloat16)
    value_update = jnp.dot(basis, normalized, preferred_element_type=jnp.float32).astype(jnp.bfloat16)
    return (new_first, new_second, value_update)
```

```python
import math

import jax
import jax.numpy as jnp
from jax import lax
from jax.sharding import Mesh
from jax.sharding import PartitionSpec as P

STEP = 1000

beta_first = 0.9
beta_second = 0.999
adam_epsilon = 1e-08

AXES = ("z_lo", "x", "y", "z_hi", "core")
Z = ("z_hi", "z_lo")
RANK = 512
TOKENS = 65536


def owner_row(core, xy, z):
    x, y = xy // 4, xy % 4
    z_hi, z_lo = z // 4, z % 4
    return (((z_lo * 4 + x) * 4 + y) * 4 + z_hi) * 2 + core


def reorder(basis, rows):
    pick = (lax.broadcasted_iota(jnp.int32, (RANK, RANK), 0) == rows[None, :]).astype(jnp.bfloat16)
    return jnp.dot(basis, pick, preferred_element_type=jnp.float32).astype(jnp.bfloat16)


def shifts(block, axis):
    return [block] + [
        lax.ppermute(block, axis, [(i, (i + k) % 4) for i in range(4)]) for k in (1, 2, 3)
    ]


def ordered(parts, index):
    stacked = jnp.stack(parts)
    return jnp.take(stacked, (index - jnp.arange(4)) % 4, axis=0)


def local(normed_input, value_cotangent, basis, first_moment, second_moment):
    x_at, y_at, z_lo_at = lax.axis_index("x"), lax.axis_index("y"), lax.axis_index("z_lo")
    place = jnp.arange(RANK)
    with jax.named_scope("order"):
        ranked = reorder(basis, owner_row(place // 256, place // 16 % 16, place % 16))
        decoder = reorder(basis, owner_row(place // 16 % 2, place // 32, place % 16))
    with jax.named_scope("swap_tokens"):
        swap = [(0, 1), (1, 0)]
        other_input = lax.ppermute(normed_input, "core", swap)
        other_cotangent = lax.ppermute(value_cotangent, "core", swap)
    with jax.named_scope("gather_z"):
        mine = lax.dynamic_slice_in_dim(ranked, (x_at * 4 + z_lo_at) * 16, 16, 0)
        halves = jnp.stack([mine[:, :256], mine[:, 256:]])
        line = lax.all_to_all(
            jnp.broadcast_to(halves[None], (16, 2, 16, 256)).reshape(32, 16, 256),
            ("z_hi", "z_lo", "core"), 0, 0, tiled=True,
        ).reshape(4, 4, 2, 16, 256)
        lower, upper = line[:, :, 0], line[:, :, 1]
    with jax.named_scope("gather_xy"):
        lower_x = shifts(lower, "x")
        upper_y = shifts(upper, "y")
        lower_x = ordered(lower_x, x_at)
        upper_y = ordered(upper_y, y_at)
    with jax.named_scope("gather_yx"):
        lower_xy = shifts(lower_x, "y")
        upper_xy = shifts(upper_y, "x")
        lower_all = ordered(lower_xy, y_at).transpose(0, 2, 1, 3, 4, 5).reshape(4, 4, 256, 256)
        upper_all = ordered(upper_xy, x_at).transpose(1, 2, 0, 3, 4, 5).reshape(4, 4, 256, 256)
    with jax.named_scope("project"):
        whole = jnp.stack([lower_all, upper_all], axis=2).reshape(8192, 256)

        def term(tokens, cotangent):
            reduced = jnp.dot(tokens, whole, preferred_element_type=jnp.float32)
            high = lax.reduce_precision(reduced, 8, 7)
            low = (reduced - high).astype(jnp.bfloat16)
            both = jnp.concatenate([high.astype(jnp.bfloat16), low], axis=0)
            twice = jnp.concatenate([cotangent, cotangent], axis=0)
            return lax.dot_general(
                both, twice, (((0,), (0,)), ((), ())), preferred_element_type=jnp.float32
            )

        partial = term(normed_input, value_cotangent) + term(other_input, other_cotangent)
    with jax.named_scope("reduce_xy"):
        parts = lax.all_to_all(partial.reshape(16, 16, 1024), ("x", "y"), 0, 0, tiled=True)
        summed = jnp.sum(parts, axis=0)
    with jax.named_scope("reduce_z"):
        parts = lax.all_to_all(summed.reshape(16, 8, 128), Z, 0, 0, tiled=True)
        share = jnp.sum(parts, axis=0) * (1.0 / math.sqrt(TOKENS))
    with jax.named_scope("adam"):
        first, second = first_moment.reshape(8, 128), second_moment.reshape(8, 128)
        new_first = beta_first * first + (1.0 - beta_first) * share
        new_second = beta_second * second + (1.0 - beta_second) * share * share
        corr_first = 1.0 - beta_first**STEP
        corr_second = 1.0 - beta_second**STEP
        normalized = (
            new_first / corr_first / (jnp.sqrt(new_second / corr_second) + adam_epsilon)
        ).astype(jnp.bfloat16)
    with jax.named_scope("spread_z"):
        column = lax.all_gather(normalized, Z, axis=0, tiled=False).reshape(16, 1024)
    with jax.named_scope("spread_xy"):
        step = lax.all_to_all(
            jnp.broadcast_to(column[None], (32, 16, 1024)), ("x", "y", "core"), 0, 0, tiled=True
        ).reshape(RANK, 1024)
    with jax.named_scope("decode"):
        update = jnp.dot(decoder, step, preferred_element_type=jnp.float32).astype(jnp.bfloat16)
    return new_first.reshape(1, 1024), new_second.reshape(1, 1024), update


def solution(mesh):
    fine = Mesh(mesh.devices.reshape(4, 4, 4, 4, 2), AXES)
    weights = P(("y", "z_hi", "core"), None)
    return jax.shard_map(
        local,
        mesh=fine,
        in_specs=(P(AXES, None), P(AXES, None), weights, P(AXES, None), P(AXES, None)),
        out_specs=(P(AXES, None), P(AXES, None), weights),
        check_vma=False,
    )
```

```python
import math

import jax
import jax.numpy as jnp
from jax import lax
from jax.sharding import Mesh
from jax.sharding import PartitionSpec as P

STEP = 1000

beta_first = 0.9
beta_second = 0.999
adam_epsilon = 1e-08

AXES = ("z_lo", "x", "y", "z_hi", "core")
Z = ("z_hi", "z_lo")
RANK = 512
TOKENS = 65536


def owner_row(core, xy, z):
    x, y = xy // 4, xy % 4
    z_hi, z_lo = z // 4, z % 4
    return (((z_lo * 4 + x) * 4 + y) * 4 + z_hi) * 2 + core


def reorder(basis, rows):
    pick = (lax.broadcasted_iota(jnp.int32, (RANK, RANK), 0) == rows[None, :]).astype(jnp.bfloat16)
    return jnp.dot(basis, pick, preferred_element_type=jnp.float32).astype(jnp.bfloat16)


def exchange(blocks, axes):
    return lax.all_to_all(blocks, axes, 0, 0, tiled=True)


def spread(block, axes, count):
    return exchange(jnp.broadcast_to(block[None], (count, *block.shape)), axes)


def quarter(tokens, at):
    return lax.dynamic_index_in_dim(
        tokens.reshape(128, 16, 4, 128), (at & 1) * 2 + (at >> 1), 2, keepdims=False
    ).reshape(128, 2048)


def local(normed_input, value_cotangent, basis, first_moment, second_moment):
    x_at, z_lo_at, core_at = (lax.axis_index(a) for a in ("x", "z_lo", "core"))
    swap = [(0, 1), (1, 0)]
    place = jnp.arange(RANK)
    with jax.named_scope("order"):
        ranked = reorder(basis, owner_row(place // 256, place // 16 % 16, place % 16))
        decoder = reorder(basis, owner_row(place // 16 % 2, place // 32, place % 16))
    with jax.named_scope("tokens_x"):
        pieces = [
            jnp.concatenate([quarter(normed_input, (x_at + k) & 3), value_cotangent], axis=1)
            for k in range(4)
        ]
        pieces = pieces[:1] + [
            lax.ppermute(pieces[k], "x", [(i, (i + k) % 4) for i in range(4)]) for k in (1, 3, 2)
        ]
    with jax.named_scope("tokens_core"):
        pieces += [lax.ppermute(piece, "core", swap) for piece in pieces]
    with jax.named_scope("gather_core"):
        rows = lax.dynamic_slice_in_dim(ranked, (x_at >> 1) * 128 + z_lo_at * 32, 32, 0)
        low, high = rows[:, :256], rows[:, 256:]
        theirs = lax.ppermute(jnp.where(core_at == 0, high, low), "core", swap)
        chunk = jnp.where(core_at == (x_at & 1), jnp.where(core_at == 0, low, high), theirs)
    with jax.named_scope("gather_z"):
        line = spread(chunk, Z, 16).reshape(512, 256)
    with jax.named_scope("gather_y"):
        whole = spread(line, "y", 4).reshape(2048, 256)
    with jax.named_scope("project"):
        reduced = jnp.concatenate(
            [
                jnp.dot(piece[:, :2048], whole, preferred_element_type=jnp.float32)
                for piece in pieces
            ]
        )
        cotangents = jnp.concatenate([piece[:, 2048:] for piece in pieces])
        high = lax.reduce_precision(reduced, 8, 7)
        low = (reduced - high).astype(jnp.bfloat16)
        partial = sum(
            lax.dot_general(
                part, cotangents, (((0,), (0,)), ((), ())), preferred_element_type=jnp.float32
            )
            for part in (high.astype(jnp.bfloat16), low)
        )
    with jax.named_scope("reduce_xy"):
        parts = exchange(partial.reshape(16, 16, 1024), ("x", "y"))
        summed = jnp.sum(parts, axis=0)
    with jax.named_scope("reduce_z"):
        parts = exchange(summed.reshape(16, 8, 128), Z)
        share = jnp.sum(parts, axis=0) * (1.0 / math.sqrt(TOKENS))
    with jax.named_scope("adam"):
        first, second = first_moment.reshape(8, 128), second_moment.reshape(8, 128)
        new_first = beta_first * first + (1.0 - beta_first) * share
        new_second = beta_second * second + (1.0 - beta_second) * share * share
        corr_first = 1.0 - beta_first**STEP
        corr_second = 1.0 - beta_second**STEP
        normalized = (
            new_first / corr_first / (jnp.sqrt(new_second / corr_second) + adam_epsilon)
        ).astype(jnp.bfloat16)
    with jax.named_scope("spread_z"):
        column = spread(normalized, Z, 16).reshape(16, 1024)
    with jax.named_scope("spread_xy"):
        step = spread(column, ("x", "y", "core"), 32).reshape(RANK, 1024)
    with jax.named_scope("decode"):
        update = jnp.dot(decoder, step, preferred_element_type=jnp.float32).astype(jnp.bfloat16)
    return new_first.reshape(1, 1024), new_second.reshape(1, 1024), update


def solution(mesh):
    fine = Mesh(mesh.devices.reshape(4, 4, 4, 4, 2), AXES)
    weights = P(("y", "z_hi", "core"), None)
    return jax.shard_map(
        local,
        mesh=fine,
        in_specs=(P(AXES, None), P(AXES, None), weights, P(AXES, None), P(AXES, None)),
        out_specs=(P(AXES, None), P(AXES, None), weights),
        check_vma=False,
    )
```

```python
import math

import jax
import jax.numpy as jnp
from jax import lax
from jax.experimental import pallas as pl
from jax.experimental.pallas import tpu as pltpu
from jax.sharding import Mesh
from jax.sharding import PartitionSpec as P

STEP = 1000

beta_first = 0.9
beta_second = 0.999
adam_epsilon = 1e-08

AXES = ("z_lo", "x", "y", "z_hi", "core")
RANK = 512
TOKENS = 65536
KVW = 1024
QUARTER = 2048


def reorder(basis, rows):
    pick = (lax.broadcasted_iota(jnp.int32, (RANK, RANK), 0) == rows[None, :]).astype(jnp.bfloat16)
    return jnp.dot(basis, pick, preferred_element_type=jnp.float32).astype(jnp.bfloat16)


def exchange(blocks, axes):
    return lax.all_to_all(blocks, axes, 0, 0, tiled=True)


def spread(block, axes, count):
    return exchange(jnp.broadcast_to(block[None], (count, *block.shape)), axes)


def pack_kernel(x_ref, tokens_ref, cotangent_ref, *out_refs):
    for k, out_ref in enumerate(out_refs):
        at = (x_ref[0] + k) & 3
        offset = pl.multiple_of((at & 1) * 256 + (at >> 1) * 128, 128)
        for block in range(16):
            out_ref[:, block * 128 : block * 128 + 128] = tokens_ref[
                :, pl.ds(pl.multiple_of(block * 512 + offset, 128), 128)
            ]
        out_ref[:, QUARTER:] = cotangent_ref[...]


def pack(x_at, tokens, cotangent):
    rows = 32
    return pl.pallas_call(
        pack_kernel,
        grid=(128 // rows,),
        in_specs=[
            pl.BlockSpec(memory_space=pltpu.SMEM),
            pl.BlockSpec((rows, 8192), lambda i: (i, 0)),
            pl.BlockSpec((rows, KVW), lambda i: (i, 0)),
        ],
        out_specs=[pl.BlockSpec((rows, QUARTER + KVW), lambda i: (i, 0))] * 4,
        out_shape=[jax.ShapeDtypeStruct((128, QUARTER + KVW), jnp.bfloat16)] * 4,
        compiler_params=pltpu.CompilerParams(vmem_limit_bytes=32 * 2**20),
        cost_estimate=pl.CostEstimate(flops=0, bytes_accessed=6 * 2**20, transcendentals=0),
        name="pack",
    )(x_at[None], tokens, cotangent)


def project_kernel(*refs):
    *pieces, whole_ref, out_ref, split_ref = refs
    whole = whole_ref[...]
    count = len(pieces)
    for k, piece in enumerate(pieces):
        reduced = jnp.dot(piece[:, :QUARTER], whole, preferred_element_type=jnp.float32)
        high = reduced.astype(jnp.bfloat16)
        low = (reduced - high.astype(jnp.float32)).astype(jnp.bfloat16)
        split_ref[k * 128 : k * 128 + 128] = high
        split_ref[(count + k) * 128 : (count + k) * 128 + 128] = low
    for n in range(0, KVW, 256):
        columns = [piece[:, QUARTER + n : QUARTER + n + 256] for piece in pieces]
        out_ref[:, n : n + 256] = lax.dot_general(
            split_ref[...],
            jnp.concatenate(columns + columns, axis=0),
            (((0,), (0,)), ((), ())),
            preferred_element_type=jnp.float32,
        ).astype(jnp.bfloat16)


def project(pieces, whole):
    vmem = pl.BlockSpec(memory_space=pltpu.VMEM)
    return pl.pallas_call(
        project_kernel,
        in_specs=[vmem] * (len(pieces) + 1),
        out_specs=vmem,
        out_shape=jax.ShapeDtypeStruct((256, KVW), jnp.bfloat16),
        scratch_shapes=[pltpu.VMEM((2 * 128 * len(pieces), 256), jnp.bfloat16)],
        compiler_params=pltpu.CompilerParams(vmem_limit_bytes=40 * 2**20),
        cost_estimate=pl.CostEstimate(
            flops=2 * 2**30, bytes_accessed=8 * 2**20, transcendentals=0
        ),
        name="project",
    )(*pieces, whole)


def local(normed_input, value_cotangent, basis, first_moment, second_moment):
    x_at, z_hi_at, z_lo_at, core_at = (lax.axis_index(a) for a in ("x", "z_hi", "z_lo", "core"))
    swap = [(0, 1), (1, 0)]
    place = jnp.arange(RANK)
    with jax.named_scope("order"):
        ranked = reorder(basis, (place & 255) * 2 + (place >> 8))
        decoder = reorder(basis, (place & ~7) + (place & 3) * 2 + (place >> 2 & 1))
    with jax.named_scope("gather_core"):
        rows = lax.dynamic_slice_in_dim(ranked, (x_at >> 1) * 128 + z_lo_at * 32, 32, 0)
        low, high = rows[:, :256], rows[:, 256:]
        theirs = lax.ppermute(jnp.where(core_at == 0, high, low), "core", swap)
        chunk = jnp.where(core_at == (x_at & 1), jnp.where(core_at == 0, low, high), theirs)
    with jax.named_scope("tokens_x"):
        packed = pack(x_at, normed_input, value_cotangent)
        pieces = [packed[0]] + [
            lax.ppermute(packed[k], "x", [(i, (i + k) % 4) for i in range(4)]) for k in (1, 3, 2)
        ]
    with jax.named_scope("tokens_core"):
        pieces += [lax.ppermute(piece, "core", swap) for piece in pieces]
    with jax.named_scope("gather_z"):
        line = spread(chunk, ("z_hi", "z_lo"), 16).reshape(512, 256)
    with jax.named_scope("gather_y"):
        whole = spread(line, "y", 4).reshape(QUARTER, 256)
    with jax.named_scope("moments_z"):
        own = jnp.concatenate([first_moment, second_moment])
        row = lax.broadcasted_iota(jnp.int32, (4, KVW), 0)
        first = second = jnp.zeros((4, KVW), jnp.float32)
        for k in range(4):
            theirs = lax.ppermute(own, "z_hi", [(i, (i + k) % 4) for i in range(4)]) if k else own
            place_of = row == ((z_hi_at - k) & 3)
            first = jnp.where(place_of, theirs[:1], first)
            second = jnp.where(place_of, theirs[1:], second)
    with jax.named_scope("project"):
        partial = project(pieces, whole)
    with jax.named_scope("reduce_plane"):
        parts = exchange(partial.reshape(64, 4, KVW), ("z_lo", "x", "y"))
        summed = jnp.sum(parts.astype(jnp.float32), axis=0)
    with jax.named_scope("reduce_z"):
        share = jnp.sum(spread(summed, "z_hi", 4), axis=0) * (1.0 / math.sqrt(TOKENS))
    with jax.named_scope("adam"):
        new_first = beta_first * first + (1.0 - beta_first) * share
        new_second = beta_second * second + (1.0 - beta_second) * share * share
        corr_first = 1.0 - beta_first**STEP
        corr_second = 1.0 - beta_second**STEP
        normalized = (
            new_first / corr_first / (jnp.sqrt(new_second / corr_second) + adam_epsilon)
        ).astype(jnp.bfloat16)
    with jax.named_scope("spread_plane"):
        step = spread(normalized, ("z_lo", "x", "y", "core"), 128).reshape(RANK, KVW)
    with jax.named_scope("decode"):
        update = jnp.dot(decoder, step, preferred_element_type=jnp.float32).astype(jnp.bfloat16)
    with jax.named_scope("own"):
        own_first = lax.dynamic_slice_in_dim(new_first, z_hi_at, 1, 0)
        own_second = lax.dynamic_slice_in_dim(new_second, z_hi_at, 1, 0)
    return own_first, own_second, update


def solution(mesh):
    fine = Mesh(mesh.devices.reshape(4, 4, 4, 4, 2), AXES)
    weights = P(("y", "z_hi", "core"), None)
    return jax.shard_map(
        local,
        mesh=fine,
        in_specs=(P(AXES, None), P(AXES, None), weights, P(AXES, None), P(AXES, None)),
        out_specs=(P(AXES, None), P(AXES, None), weights),
        check_vma=False,
    )
```

```python
import math

import jax
import jax.numpy as jnp
from jax import lax
from jax.experimental import pallas as pl
from jax.experimental.pallas import tpu as pltpu
from jax.sharding import Mesh
from jax.sharding import PartitionSpec as P

STEP = 1000

beta_first = 0.9
beta_second = 0.999
adam_epsilon = 1e-08

AXES = ("z_lo", "x", "y", "z_hi", "core")
Z = ("z_hi", "z_lo")
RANK = 512
TOKENS = 65536
KVW = 1024
QUARTER = 2048


def owner_row(core, xy, z):
    x, y = xy >> 2, xy & 3
    z_hi, z_lo = z >> 2, z & 3
    return (((z_lo * 4 + x) * 4 + y) * 4 + z_hi) * 2 + core


def reorder(basis, rows):
    pick = (lax.broadcasted_iota(jnp.int32, (RANK, RANK), 0) == rows[None, :]).astype(jnp.bfloat16)
    return jnp.dot(basis, pick, preferred_element_type=jnp.float32).astype(jnp.bfloat16)


def exchange(blocks, axes):
    return lax.all_to_all(blocks, axes, 0, 0, tiled=True)


def spread(block, axes, count):
    return exchange(jnp.broadcast_to(block[None], (count, *block.shape)), axes)


def pack_kernel(x_ref, tokens_ref, cotangent_ref, *out_refs):
    for k, out_ref in enumerate(out_refs):
        at = (x_ref[0] + k) & 3
        offset = pl.multiple_of((at & 1) * 256 + (at >> 1) * 128, 128)
        for block in range(16):
            out_ref[:, block * 128 : block * 128 + 128] = tokens_ref[
                :, pl.ds(pl.multiple_of(block * 512 + offset, 128), 128)
            ]
        out_ref[:, QUARTER:] = cotangent_ref[...]


def pack(x_at, tokens, cotangent):
    rows = 32
    return pl.pallas_call(
        pack_kernel,
        grid=(128 // rows,),
        in_specs=[
            pl.BlockSpec(memory_space=pltpu.SMEM),
            pl.BlockSpec((rows, 8192), lambda i: (i, 0)),
            pl.BlockSpec((rows, KVW), lambda i: (i, 0)),
        ],
        out_specs=[pl.BlockSpec((rows, QUARTER + KVW), lambda i: (i, 0))] * 4,
        out_shape=[jax.ShapeDtypeStruct((128, QUARTER + KVW), jnp.bfloat16)] * 4,
        compiler_params=pltpu.CompilerParams(vmem_limit_bytes=32 * 2**20),
        cost_estimate=pl.CostEstimate(flops=0, bytes_accessed=6 * 2**20, transcendentals=0),
        name="pack",
    )(x_at[None], tokens, cotangent)


def join_kernel(*refs):
    *pieces, _, out_ref = refs
    for k, piece in enumerate(pieces):
        rows = piece.shape[0]
        out_ref[k * rows : k * rows + rows] = piece[...]


def join(pieces, other):
    rows, columns = pieces[0].shape
    vmem = pl.BlockSpec(memory_space=pltpu.VMEM)
    return pl.pallas_call(
        join_kernel,
        in_specs=[vmem] * len(pieces) + [pl.BlockSpec(memory_space=pl.ANY)],
        out_specs=vmem,
        out_shape=jax.ShapeDtypeStruct((rows * len(pieces), columns), jnp.bfloat16),
        compiler_params=pltpu.CompilerParams(vmem_limit_bytes=16 * 2**20),
        cost_estimate=pl.CostEstimate(flops=0, bytes_accessed=2**20, transcendentals=0),
        name="join",
    )(*pieces, other)


def project_kernel(*refs):
    *pieces, whole_ref, out_ref, split_ref = refs
    whole = whole_ref[...]
    at, tokens = 0, split_ref.shape[0] // 2
    for piece in pieces:
        rows = piece.shape[0]
        reduced = jnp.dot(piece[:, :QUARTER], whole, preferred_element_type=jnp.float32)
        high = reduced.astype(jnp.bfloat16)
        low = (reduced - high.astype(jnp.float32)).astype(jnp.bfloat16)
        split_ref[at : at + rows] = high
        split_ref[tokens + at : tokens + at + rows] = low
        at += rows
    for n in range(0, KVW, 256):
        columns = [piece[:, QUARTER + n : QUARTER + n + 256] for piece in pieces]
        out_ref[:, n : n + 256] = lax.dot_general(
            split_ref[...],
            jnp.concatenate(columns + columns, axis=0),
            (((0,), (0,)), ((), ())),
            preferred_element_type=jnp.float32,
        )


def project(pieces, whole):
    vmem = pl.BlockSpec(memory_space=pltpu.VMEM)
    return pl.pallas_call(
        project_kernel,
        in_specs=[vmem] * (len(pieces) + 1),
        out_specs=vmem,
        out_shape=jax.ShapeDtypeStruct((256, KVW), jnp.float32),
        scratch_shapes=[pltpu.VMEM((2048, 256), jnp.bfloat16)],
        compiler_params=pltpu.CompilerParams(vmem_limit_bytes=40 * 2**20),
        cost_estimate=pl.CostEstimate(
            flops=2 * 2**30, bytes_accessed=8 * 2**20, transcendentals=0
        ),
        name="project",
    )(*pieces, whole)


def local(normed_input, value_cotangent, basis, first_moment, second_moment):
    x_at, z_lo_at, core_at = (lax.axis_index(a) for a in ("x", "z_lo", "core"))
    swap = [(0, 1), (1, 0)]
    place = jnp.arange(RANK)
    with jax.named_scope("order"):
        ranked = reorder(basis, owner_row(place >> 8, place >> 4 & 15, place & 15))
        decoder = reorder(basis, owner_row(place >> 4 & 1, place >> 5, place & 15))
    with jax.named_scope("gather_core"):
        rows = lax.dynamic_slice_in_dim(ranked, (x_at >> 1) * 128 + z_lo_at * 32, 32, 0)
        low, high = rows[:, :256], rows[:, 256:]
        theirs = lax.ppermute(jnp.where(core_at == 0, high, low), "core", swap)
        chunk = jnp.where(core_at == (x_at & 1), jnp.where(core_at == 0, low, high), theirs)
    with jax.named_scope("tokens_x"):
        packed = pack(x_at, normed_input, value_cotangent)
        pieces = [packed[0]] + [
            lax.ppermute(packed[k], "x", [(i, (i + k) % 4) for i in range(4)]) for k in (1, 3, 2)
        ]
    with jax.named_scope("gather_z"):
        line = spread(join([chunk], packed[1]), Z, 16).reshape(512, 256)
    with jax.named_scope("gather_y"):
        whole = spread(line, "y", 4).reshape(QUARTER, 256)
    with jax.named_scope("tokens_core"):
        held = join(pieces, whole)
        held = [held, lax.ppermute(held, "core", swap)]
    with jax.named_scope("project"):
        partial = project(held, whole)
    with jax.named_scope("reduce_xy"):
        summed = jnp.sum(exchange(partial.reshape(16, 16, KVW), ("x", "y")), axis=0)
    with jax.named_scope("reduce_z"):
        share = jnp.sum(exchange(summed.reshape(16, 8, 128), Z), axis=0)
        share = share * (1.0 / math.sqrt(TOKENS))
    with jax.named_scope("adam"):
        first, second = first_moment.reshape(8, 128), second_moment.reshape(8, 128)
        new_first = beta_first * first + (1.0 - beta_first) * share
        new_second = beta_second * second + (1.0 - beta_second) * share * share
        corr_first = 1.0 - beta_first**STEP
        corr_second = 1.0 - beta_second**STEP
        normalized = (
            new_first / corr_first / (jnp.sqrt(new_second / corr_second) + adam_epsilon)
        ).astype(jnp.bfloat16)
    with jax.named_scope("spread_z"):
        column = spread(normalized, Z, 16).reshape(16, KVW)
    with jax.named_scope("spread_xy"):
        step = spread(column, ("x", "y", "core"), 32).reshape(RANK, KVW)
    with jax.named_scope("decode"):
        update = jnp.dot(decoder, step, preferred_element_type=jnp.float32).astype(jnp.bfloat16)
    return new_first.reshape(1, KVW), new_second.reshape(1, KVW), update


def solution(mesh):
    fine = Mesh(mesh.devices.reshape(4, 4, 4, 4, 2), AXES)
    weights = P(("y", "z_hi", "core"), None)
    return jax.shard_map(
        local,
        mesh=fine,
        in_specs=(P(AXES, None), P(AXES, None), weights, P(AXES, None), P(AXES, None)),
        out_specs=(P(AXES, None), P(AXES, None), weights),
        check_vma=False,
    )
```

```python
import math

import jax
import jax.numpy as jnp
import numpy as np
from jax import lax
from jax.experimental import pallas as pl
from jax.experimental.pallas import tpu as pltpu
from jax.sharding import Mesh
from jax.sharding import PartitionSpec as P

STEP = 1000

beta_first = 0.9
beta_second = 0.999
adam_epsilon = 1e-08

AXES = ("z_lo", "x", "y", "z_hi", "core")
Z = ("z_hi", "z_lo")
RANK = 512
TOKENS = 65536
KVW = 1024
QUARTER = 2048


def owner_row(core, xy, z):
    x, y = xy >> 2, xy & 3
    z_hi, z_lo = z >> 2, z & 3
    return (((z_lo * 4 + x) * 4 + y) * 4 + z_hi) * 2 + core


def reorder(basis, rows):
    pick = (lax.broadcasted_iota(jnp.int32, (RANK, RANK), 0) == rows[None, :]).astype(jnp.bfloat16)
    return jnp.dot(basis, pick, preferred_element_type=jnp.float32).astype(jnp.bfloat16)


def exchange(blocks, axes):
    return lax.all_to_all(blocks, axes, 0, 0, tiled=True)


def spread(block, axes, count):
    return exchange(jnp.broadcast_to(block[None], (count, *block.shape)), axes)


def pack_kernel(x_ref, tokens_ref, cotangent_ref, *out_refs):
    for k, out_ref in enumerate(out_refs):
        at = (x_ref[0] + k) & 3
        offset = pl.multiple_of((at & 1) * 256 + (at >> 1) * 128, 128)
        for block in range(16):
            out_ref[:, block * 128 : block * 128 + 128] = tokens_ref[
                :, pl.ds(pl.multiple_of(block * 512 + offset, 128), 128)
            ]
        out_ref[:, QUARTER:] = cotangent_ref[...]


def pack(x_at, tokens, cotangent):
    rows = 32
    return pl.pallas_call(
        pack_kernel,
        grid=(128 // rows,),
        in_specs=[
            pl.BlockSpec(memory_space=pltpu.SMEM),
            pl.BlockSpec((rows, 8192), lambda i: (i, 0)),
            pl.BlockSpec((rows, KVW), lambda i: (i, 0)),
        ],
        out_specs=[pl.BlockSpec((rows, QUARTER + KVW), lambda i: (i, 0))] * 4,
        out_shape=[jax.ShapeDtypeStruct((128, QUARTER + KVW), jnp.bfloat16)] * 4,
        compiler_params=pltpu.CompilerParams(vmem_limit_bytes=32 * 2**20),
        cost_estimate=pl.CostEstimate(flops=0, bytes_accessed=6 * 2**20, transcendentals=0),
        name="pack",
    )(x_at[None], tokens, cotangent)


def join_kernel(*refs):
    *pieces, _, out_ref = refs
    for k, piece in enumerate(pieces):
        rows = piece.shape[0]
        out_ref[k * rows : k * rows + rows] = piece[...]


def join(pieces, other):
    rows, columns = pieces[0].shape
    vmem = pl.BlockSpec(memory_space=pltpu.VMEM)
    return pl.pallas_call(
        join_kernel,
        in_specs=[vmem] * len(pieces) + [pl.BlockSpec(memory_space=pl.ANY)],
        out_specs=vmem,
        out_shape=jax.ShapeDtypeStruct((rows * len(pieces), columns), jnp.bfloat16),
        compiler_params=pltpu.CompilerParams(vmem_limit_bytes=16 * 2**20),
        cost_estimate=pl.CostEstimate(flops=0, bytes_accessed=2**20, transcendentals=0),
        name="join",
    )(*pieces, other)


def project_kernel(*refs):
    *pieces, whole_ref, out_ref, split_ref = refs
    whole = whole_ref[...]
    at, tokens = 0, split_ref.shape[0] // 2
    for piece in pieces:
        rows = piece.shape[0]
        reduced = jnp.dot(piece[:, :QUARTER], whole, preferred_element_type=jnp.float32)
        high = reduced.astype(jnp.bfloat16)
        low = (reduced - high.astype(jnp.float32)).astype(jnp.bfloat16)
        split_ref[at : at + rows] = high
        split_ref[tokens + at : tokens + at + rows] = low
        at += rows
    for n in range(0, KVW, 256):
        columns = [piece[:, QUARTER + n : QUARTER + n + 256] for piece in pieces]
        out_ref[:, n : n + 256] = lax.dot_general(
            split_ref[...],
            jnp.concatenate(columns + columns, axis=0),
            (((0,), (0,)), ((), ())),
            preferred_element_type=jnp.float32,
        )


def project(pieces, whole):
    vmem = pl.BlockSpec(memory_space=pltpu.VMEM)
    return pl.pallas_call(
        project_kernel,
        in_specs=[vmem] * (len(pieces) + 1),
        out_specs=vmem,
        out_shape=jax.ShapeDtypeStruct((256, KVW), jnp.float32),
        scratch_shapes=[pltpu.VMEM((2048, 256), jnp.bfloat16)],
        compiler_params=pltpu.CompilerParams(vmem_limit_bytes=40 * 2**20),
        cost_estimate=pl.CostEstimate(
            flops=2 * 2**30, bytes_accessed=8 * 2**20, transcendentals=0
        ),
        name="project",
    )(*pieces, whole)


def adam_kernel(parts_ref, first_hbm, second_hbm, new_first_ref, new_second_ref, normalized_ref,
                first_ref, second_ref, step_ref, semaphores):
    fetches = [
        pltpu.make_async_copy(first_hbm, first_ref, semaphores.at[0]),
        pltpu.make_async_copy(second_hbm, second_ref, semaphores.at[1]),
    ]
    for fetch in fetches:
        fetch.start()
    shares = jnp.sum(parts_ref[...], axis=0) * (1.0 / math.sqrt(TOKENS))
    for fetch in fetches:
        fetch.wait()
    corr_first = 1.0 - beta_first**STEP
    corr_second = 1.0 - beta_second**STEP
    for n in range(8):
        columns = slice(n * 128, n * 128 + 128)
        share = shares[n : n + 1]
        new_first = beta_first * first_ref[:, columns] + (1.0 - beta_first) * share
        new_second = beta_second * second_ref[:, columns] + (1.0 - beta_second) * share * share
        new_first_ref[:, columns] = new_first
        new_second_ref[:, columns] = new_second
        step_ref[n : n + 1] = (
            new_first / corr_first / (jnp.sqrt(new_second / corr_second) + adam_epsilon)
        )
    normalized_ref[...] = step_ref[...].astype(jnp.bfloat16)


def adam(parts, first, second):
    vmem, anywhere = pl.BlockSpec(memory_space=pltpu.VMEM), pl.BlockSpec(memory_space=pl.ANY)
    row = jax.ShapeDtypeStruct((1, KVW), jnp.float32)
    return pl.pallas_call(
        adam_kernel,
        in_specs=[vmem, anywhere, anywhere],
        out_specs=[vmem] * 3,
        out_shape=[row, row, jax.ShapeDtypeStruct((8, 128), jnp.bfloat16)],
        scratch_shapes=[
            pltpu.VMEM((1, KVW), jnp.float32),
            pltpu.VMEM((1, KVW), jnp.float32),
            pltpu.VMEM((8, 128), jnp.float32),
            pltpu.SemaphoreType.DMA((2,)),
        ],
        compiler_params=pltpu.CompilerParams(vmem_limit_bytes=48 * 2**20),
        cost_estimate=pl.CostEstimate(flops=2**14, bytes_accessed=2**16, transcendentals=2**10),
        name="adam",
    )(parts, first, second)


def local(normed_input, value_cotangent, basis, first_moment, second_moment):
    x_at, z_lo_at, core_at = (lax.axis_index(a) for a in ("x", "z_lo", "core"))
    swap = [(0, 1), (1, 0)]
    place = np.arange(RANK, dtype=np.int32)
    with jax.named_scope("order"):
        ranked = reorder(basis, owner_row(place >> 8, place >> 4 & 15, place & 15))
        decoder = reorder(basis, owner_row(place >> 4 & 1, place >> 5, place & 15))
    with jax.named_scope("tokens_x"):
        packed = pack(x_at, normed_input, value_cotangent)
        pieces = [packed[0]] + [
            lax.ppermute(packed[k], "x", [(i, (i + k) % 4) for i in range(4)]) for k in (1, 3, 2)
        ]
    with jax.named_scope("gather_core"):
        rows = lax.dynamic_slice_in_dim(ranked, (x_at >> 1) * 128 + z_lo_at * 32, 32, 0)
        rows = join([rows], packed[1])
        low, high = rows[:, :256], rows[:, 256:]
        theirs = lax.ppermute(jnp.where(core_at == 0, high, low), "core", swap)
        chunk = jnp.where(core_at == (x_at & 1), jnp.where(core_at == 0, low, high), theirs)
    with jax.named_scope("gather_z"):
        line = spread(chunk, Z, 16).reshape(512, 256)
    with jax.named_scope("gather_y"):
        whole = spread(line, "y", 4).reshape(QUARTER, 256)
    with jax.named_scope("tokens_core"):
        held = join(pieces, whole)
        held = [held, lax.ppermute(held, "core", swap)]
    with jax.named_scope("project"):
        partial = project(held, whole)
    with jax.named_scope("reduce_xy"):
        summed = jnp.sum(exchange(partial.reshape(16, 16, KVW), ("x", "y")), axis=0)
    with jax.named_scope("reduce_z"):
        parts = exchange(summed.reshape(16, 8, 128), Z)
    with jax.named_scope("adam"):
        new_first, new_second, normalized = adam(parts, first_moment, second_moment)
    with jax.named_scope("spread_z"):
        column = spread(normalized, Z, 16).reshape(16, KVW)
    with jax.named_scope("spread_xy"):
        step = spread(column, ("x", "y", "core"), 32).reshape(RANK, KVW)
    with jax.named_scope("decode"):
        update = jnp.dot(decoder, step, preferred_element_type=jnp.float32).astype(jnp.bfloat16)
    return new_first, new_second, update


def solution(mesh):
    fine = Mesh(mesh.devices.reshape(4, 4, 4, 4, 2), AXES)
    weights = P(("y", "z_hi", "core"), None)
    return jax.shard_map(
        local,
        mesh=fine,
        in_specs=(P(AXES, None), P(AXES, None), weights, P(AXES, None), P(AXES, None)),
        out_specs=(P(AXES, None), P(AXES, None), weights),
        check_vma=False,
    )
```

```python
import math

import jax
import jax.numpy as jnp
import numpy as np
from jax import lax
from jax.experimental import pallas as pl
from jax.experimental.pallas import tpu as pltpu
from jax.sharding import Mesh
from jax.sharding import PartitionSpec as P

STEP = 1000

beta_first = 0.9
beta_second = 0.999
adam_epsilon = 1e-08

AXES = ("z_lo", "x", "y", "z_hi", "core")
Z = ("z_hi", "z_lo")
RANK = 512
TOKENS = 65536
KVW = 1024
QUARTER = 2048


def owner_row(core, xy, z):
    x, y = xy >> 2, xy & 3
    z_hi, z_lo = z >> 2, z & 3
    return (((z_lo * 4 + x) * 4 + y) * 4 + z_hi) * 2 + core


def reorder(basis, rows):
    pick = (lax.broadcasted_iota(jnp.int32, (RANK, RANK), 0) == rows[None, :]).astype(jnp.bfloat16)
    return jnp.dot(basis, pick, preferred_element_type=jnp.float32).astype(jnp.bfloat16)


def exchange(blocks, axes):
    return lax.all_to_all(blocks, axes, 0, 0, tiled=True)


def spread(block, axes, count):
    return exchange(jnp.broadcast_to(block[None], (count, *block.shape)), axes)


def pack_kernel(x_ref, tokens_ref, cotangent_ref, *out_refs):
    for k, out_ref in enumerate(out_refs):
        at = (x_ref[0] + k) & 3
        offset = pl.multiple_of((at & 1) * 256 + (at >> 1) * 128, 128)
        for block in range(16):
            out_ref[:, block * 128 : block * 128 + 128] = tokens_ref[
                :, pl.ds(pl.multiple_of(block * 512 + offset, 128), 128)
            ]
        out_ref[:, QUARTER:] = cotangent_ref[...]


def pack(x_at, tokens, cotangent):
    rows = 32
    return pl.pallas_call(
        pack_kernel,
        grid=(128 // rows,),
        in_specs=[
            pl.BlockSpec(memory_space=pltpu.SMEM),
            pl.BlockSpec((rows, 8192), lambda i: (i, 0)),
            pl.BlockSpec((rows, KVW), lambda i: (i, 0)),
        ],
        out_specs=[pl.BlockSpec((rows, QUARTER + KVW), lambda i: (i, 0))] * 4,
        out_shape=[jax.ShapeDtypeStruct((128, QUARTER + KVW), jnp.bfloat16)] * 4,
        compiler_params=pltpu.CompilerParams(vmem_limit_bytes=32 * 2**20),
        cost_estimate=pl.CostEstimate(flops=0, bytes_accessed=6 * 2**20, transcendentals=0),
        name="pack",
    )(x_at[None], tokens, cotangent)


def join_kernel(*refs):
    *pieces, _, out_ref = refs
    for k, piece in enumerate(pieces):
        rows = piece.shape[0]
        out_ref[k * rows : k * rows + rows] = piece[...]


def join(pieces, other):
    rows, columns = pieces[0].shape
    vmem = pl.BlockSpec(memory_space=pltpu.VMEM)
    return pl.pallas_call(
        join_kernel,
        in_specs=[vmem] * len(pieces) + [pl.BlockSpec(memory_space=pl.ANY)],
        out_specs=vmem,
        out_shape=jax.ShapeDtypeStruct((rows * len(pieces), columns), jnp.bfloat16),
        compiler_params=pltpu.CompilerParams(vmem_limit_bytes=16 * 2**20),
        cost_estimate=pl.CostEstimate(flops=0, bytes_accessed=2**20, transcendentals=0),
        name="join",
    )(*pieces, other)


def project_kernel(*refs):
    *pieces, whole_ref, out_ref, split_ref = refs
    whole = whole_ref[...]
    at, tokens = 0, split_ref.shape[0] // 2
    for piece in pieces:
        rows = piece.shape[0]
        reduced = jnp.dot(piece[:, :QUARTER], whole, preferred_element_type=jnp.float32)
        high = reduced.astype(jnp.bfloat16)
        low = (reduced - high.astype(jnp.float32)).astype(jnp.bfloat16)
        split_ref[at : at + rows] = high
        split_ref[tokens + at : tokens + at + rows] = low
        at += rows
    for n in range(0, KVW, 256):
        columns = [piece[:, QUARTER + n : QUARTER + n + 256] for piece in pieces]
        out_ref[:, n : n + 256] = lax.dot_general(
            split_ref[...],
            jnp.concatenate(columns + columns, axis=0),
            (((0,), (0,)), ((), ())),
            preferred_element_type=jnp.float32,
        )


def project(pieces, whole):
    vmem = pl.BlockSpec(memory_space=pltpu.VMEM)
    return pl.pallas_call(
        project_kernel,
        in_specs=[vmem] * (len(pieces) + 1),
        out_specs=vmem,
        out_shape=jax.ShapeDtypeStruct((256, KVW), jnp.float32),
        scratch_shapes=[pltpu.VMEM((2048, 256), jnp.bfloat16)],
        compiler_params=pltpu.CompilerParams(vmem_limit_bytes=40 * 2**20),
        cost_estimate=pl.CostEstimate(
            flops=2 * 2**30, bytes_accessed=8 * 2**20, transcendentals=0
        ),
        name="project",
    )(*pieces, whole)


def adam_kernel(parts_ref, first_hbm, second_hbm, new_first_ref, new_second_ref, normalized_ref,
                first_ref, second_ref, step_ref, semaphores):
    fetches = [
        pltpu.make_async_copy(first_hbm, first_ref, semaphores.at[0]),
        pltpu.make_async_copy(second_hbm, second_ref, semaphores.at[1]),
    ]
    for fetch in fetches:
        fetch.start()
    shares = jnp.sum(parts_ref[...], axis=0) * (1.0 / math.sqrt(TOKENS))
    for fetch in fetches:
        fetch.wait()
    corr_first = 1.0 - beta_first**STEP
    corr_second = 1.0 - beta_second**STEP
    for n in range(8):
        columns = slice(n * 128, n * 128 + 128)
        share = shares[n : n + 1]
        new_first = beta_first * first_ref[:, columns] + (1.0 - beta_first) * share
        new_second = beta_second * second_ref[:, columns] + (1.0 - beta_second) * share * share
        new_first_ref[:, columns] = new_first
        new_second_ref[:, columns] = new_second
        step_ref[n : n + 1] = (
            new_first / corr_first / (jnp.sqrt(new_second / corr_second) + adam_epsilon)
        )
    normalized_ref[...] = step_ref[...].astype(jnp.bfloat16)


def adam(parts, first, second):
    vmem, anywhere = pl.BlockSpec(memory_space=pltpu.VMEM), pl.BlockSpec(memory_space=pl.ANY)
    row = jax.ShapeDtypeStruct((1, KVW), jnp.float32)
    return pl.pallas_call(
        adam_kernel,
        in_specs=[vmem, anywhere, anywhere],
        out_specs=[vmem] * 3,
        out_shape=[row, row, jax.ShapeDtypeStruct((8, 128), jnp.bfloat16)],
        scratch_shapes=[
            pltpu.VMEM((1, KVW), jnp.float32),
            pltpu.VMEM((1, KVW), jnp.float32),
            pltpu.VMEM((8, 128), jnp.float32),
            pltpu.SemaphoreType.DMA((2,)),
        ],
        compiler_params=pltpu.CompilerParams(vmem_limit_bytes=48 * 2**20),
        cost_estimate=pl.CostEstimate(flops=2**14, bytes_accessed=2**16, transcendentals=2**10),
        name="adam",
    )(parts, first, second)


def local(normed_input, value_cotangent, basis, first_moment, second_moment):
    x_at, z_lo_at, core_at = (lax.axis_index(a) for a in ("x", "z_lo", "core"))
    swap = [(0, 1), (1, 0)]
    place = np.arange(RANK, dtype=np.int32)
    with jax.named_scope("order"):
        ranked = reorder(basis, owner_row(place >> 8, place >> 4 & 15, place & 15))
        decoder = reorder(basis, owner_row(place >> 4 & 1, place >> 5, place & 15))
    with jax.named_scope("tokens_x"):
        packed = pack(x_at, normed_input, value_cotangent)
        pieces = [packed[0]] + [
            lax.ppermute(packed[k], "x", [(i, (i + k) % 4) for i in range(4)]) for k in (1, 3, 2)
        ]
    def gather(rows):
        with jax.named_scope("gather_core"):
            low, high = rows[:, :256], rows[:, 256:]
            theirs = lax.ppermute(jnp.where(core_at == 0, high, low), "core", swap)
            chunk = jnp.where(core_at == (x_at & 1), jnp.where(core_at == 0, low, high), theirs)
        with jax.named_scope("gather_z"):
            line = spread(chunk, Z, 16).reshape(512, 256)
        with jax.named_scope("gather_y"):
            return spread(line, "y", 4).reshape(QUARTER, 256)

    with jax.named_scope("gather"):
        rows = lax.dynamic_slice_in_dim(ranked, (x_at >> 1) * 128 + z_lo_at * 32, 32, 0)
        whole = lax.cond(
            x_at < 4, gather, lambda rows: jnp.zeros((QUARTER, 256), jnp.bfloat16),
            join([rows], packed[1]),
        )
    with jax.named_scope("tokens_core"):
        held = join(pieces, whole)
        held = [held, lax.ppermute(held, "core", swap)]
    with jax.named_scope("project"):
        partial = project(held, whole)
    with jax.named_scope("reduce_xy"):
        summed = jnp.sum(exchange(partial.reshape(16, 16, KVW), ("x", "y")), axis=0)
    with jax.named_scope("reduce_z"):
        parts = exchange(summed.reshape(16, 8, 128), Z)
    with jax.named_scope("adam"):
        new_first, new_second, normalized = adam(parts, first_moment, second_moment)
    with jax.named_scope("spread_z"):
        column = spread(normalized, Z, 16).reshape(16, KVW)
    with jax.named_scope("spread_xy"):
        step = spread(column, ("x", "y", "core"), 32).reshape(RANK, KVW)
    with jax.named_scope("decode"):
        update = jnp.dot(decoder, step, preferred_element_type=jnp.float32).astype(jnp.bfloat16)
    return new_first, new_second, update


def solution(mesh):
    fine = Mesh(mesh.devices.reshape(4, 4, 4, 4, 2), AXES)
    weights = P(("y", "z_hi", "core"), None)
    return jax.shard_map(
        local,
        mesh=fine,
        in_specs=(P(AXES, None), P(AXES, None), weights, P(AXES, None), P(AXES, None)),
        out_specs=(P(AXES, None), P(AXES, None), weights),
        check_vma=False,
    )
```

```python
import math

import jax
import jax.numpy as jnp
import numpy as np
from jax import lax
from jax.experimental import pallas as pl
from jax.experimental.pallas import tpu as pltpu
from jax.sharding import Mesh
from jax.sharding import PartitionSpec as P

STEP = 1000

beta_first = 0.9
beta_second = 0.999
adam_epsilon = 1e-08

AXES = ("z_lo", "x", "y", "z_hi", "core")
Z = ("z_hi", "z_lo")
RANK = 512
TOKENS = 65536
KVW = 1024
QUARTER = 2048


def owner_row(core, xy, z):
    x, y = xy >> 2, xy & 3
    z_hi, z_lo = z >> 2, z & 3
    return (((z_lo * 4 + x) * 4 + y) * 4 + z_hi) * 2 + core


def reorder(basis, rows):
    pick = (lax.broadcasted_iota(jnp.int32, (RANK, RANK), 0) == rows[None, :]).astype(jnp.bfloat16)
    return jnp.dot(basis, pick, preferred_element_type=jnp.float32).astype(jnp.bfloat16)


def exchange(blocks, axes):
    return lax.all_to_all(blocks, axes, 0, 0, tiled=True)


def spread(block, axes, count):
    return exchange(jnp.broadcast_to(block[None], (count, *block.shape)), axes)


def pack_kernel(x_ref, tokens_ref, cotangent_ref, _, *out_refs):
    for k, out_ref in enumerate(out_refs):
        at = (x_ref[0] + k) & 3
        offset = pl.multiple_of((at & 1) * 256 + (at >> 1) * 128, 128)
        for block in range(16):
            out_ref[:, block * 128 : block * 128 + 128] = tokens_ref[
                :, pl.ds(pl.multiple_of(block * 512 + offset, 128), 128)
            ]
        out_ref[:, QUARTER:] = cotangent_ref[...]


def pack(x_at, tokens, cotangent, other):
    rows = 32
    return pl.pallas_call(
        pack_kernel,
        grid=(128 // rows,),
        in_specs=[
            pl.BlockSpec(memory_space=pltpu.SMEM),
            pl.BlockSpec((rows, 8192), lambda i: (i, 0)),
            pl.BlockSpec((rows, KVW), lambda i: (i, 0)),
            pl.BlockSpec(memory_space=pl.ANY),
        ],
        out_specs=[pl.BlockSpec((rows, QUARTER + KVW), lambda i: (i, 0))] * 4,
        out_shape=[jax.ShapeDtypeStruct((128, QUARTER + KVW), jnp.bfloat16)] * 4,
        compiler_params=pltpu.CompilerParams(vmem_limit_bytes=60 * 2**20),
        cost_estimate=pl.CostEstimate(flops=0, bytes_accessed=6 * 2**20, transcendentals=0),
        name="pack",
    )(x_at[None], tokens, cotangent, other)


def join_kernel(*refs):
    *pieces, _, out_ref = refs
    for k, piece in enumerate(pieces):
        rows = piece.shape[0]
        out_ref[k * rows : k * rows + rows] = piece[...]


def join(pieces, other):
    rows, columns = pieces[0].shape
    vmem = pl.BlockSpec(memory_space=pltpu.VMEM)
    return pl.pallas_call(
        join_kernel,
        in_specs=[vmem] * len(pieces) + [pl.BlockSpec(memory_space=pl.ANY)],
        out_specs=vmem,
        out_shape=jax.ShapeDtypeStruct((rows * len(pieces), columns), jnp.bfloat16),
        compiler_params=pltpu.CompilerParams(vmem_limit_bytes=16 * 2**20),
        cost_estimate=pl.CostEstimate(flops=0, bytes_accessed=2**20, transcendentals=0),
        name="join",
    )(*pieces, other)


def project_kernel(tokens_ref, whole_ref, *refs):
    *before, out_ref, split_ref = refs
    rows = tokens_ref.shape[0]
    reduced = jnp.dot(
        tokens_ref[:, :QUARTER], whole_ref[...], preferred_element_type=jnp.float32
    )
    high = reduced.astype(jnp.bfloat16)
    split_ref[:rows] = high
    split_ref[rows:] = (reduced - high.astype(jnp.float32)).astype(jnp.bfloat16)
    for n in range(0, KVW, 256):
        cotangent = tokens_ref[:, QUARTER + n : QUARTER + n + 256]
        total = lax.dot_general(
            split_ref[...],
            jnp.concatenate([cotangent, cotangent], axis=0),
            (((0,), (0,)), ((), ())),
            preferred_element_type=jnp.float32,
        )
        for part in before:
            total += part[:, n : n + 256]
        out_ref[:, n : n + 256] = total


def project(tokens, whole, *before):
    vmem = pl.BlockSpec(memory_space=pltpu.VMEM)
    return pl.pallas_call(
        project_kernel,
        in_specs=[vmem] * (2 + len(before)),
        out_specs=vmem,
        out_shape=jax.ShapeDtypeStruct((256, KVW), jnp.float32),
        scratch_shapes=[pltpu.VMEM((1024, 256), jnp.bfloat16)],
        compiler_params=pltpu.CompilerParams(vmem_limit_bytes=24 * 2**20),
        cost_estimate=pl.CostEstimate(flops=2**30, bytes_accessed=6 * 2**20, transcendentals=0),
        name="project",
    )(tokens, whole, *before)


def decode_kernel(core_ref, basis_ref, own_ref, other_ref, out_ref):
    total = None
    for at, rows_ref in ((core_ref[0], own_ref), (1 - core_ref[0], other_ref)):
        half = basis_ref[:, pl.ds(pl.multiple_of(at * 256, 256), 256)]
        term = jnp.dot(half, rows_ref[...], preferred_element_type=jnp.float32)
        total = term if total is None else total + term
    out_ref[...] = total.astype(jnp.bfloat16)


def decode(core_at, basis, own, other):
    vmem = pl.BlockSpec(memory_space=pltpu.VMEM)
    return pl.pallas_call(
        decode_kernel,
        in_specs=[pl.BlockSpec(memory_space=pltpu.SMEM)] + [vmem] * 3,
        out_specs=vmem,
        out_shape=jax.ShapeDtypeStruct((256, KVW), jnp.bfloat16),
        compiler_params=pltpu.CompilerParams(vmem_limit_bytes=16 * 2**20),
        cost_estimate=pl.CostEstimate(flops=2**28, bytes_accessed=2**21, transcendentals=0),
        name="decode",
    )(core_at[None], basis, own, other)


def adam_kernel(parts_ref, first_hbm, second_hbm, new_first_ref, new_second_ref, normalized_ref,
                first_ref, second_ref, step_ref, semaphores):
    fetches = [
        pltpu.make_async_copy(first_hbm, first_ref, semaphores.at[0]),
        pltpu.make_async_copy(second_hbm, second_ref, semaphores.at[1]),
    ]
    for fetch in fetches:
        fetch.start()
    shares = jnp.sum(parts_ref[...], axis=0) * (1.0 / math.sqrt(TOKENS))
    for fetch in fetches:
        fetch.wait()
    corr_first = 1.0 - beta_first**STEP
    corr_second = 1.0 - beta_second**STEP
    for n in range(8):
        columns = slice(n * 128, n * 128 + 128)
        share = shares[n : n + 1]
        new_first = beta_first * first_ref[:, columns] + (1.0 - beta_first) * share
        new_second = beta_second * second_ref[:, columns] + (1.0 - beta_second) * share * share
        new_first_ref[:, columns] = new_first
        new_second_ref[:, columns] = new_second
        step_ref[n : n + 1] = (
            new_first / corr_first / (jnp.sqrt(new_second / corr_second) + adam_epsilon)
        )
    normalized_ref[...] = step_ref[...].astype(jnp.bfloat16)


def adam(parts, first, second):
    vmem, anywhere = pl.BlockSpec(memory_space=pltpu.VMEM), pl.BlockSpec(memory_space=pl.ANY)
    row = jax.ShapeDtypeStruct((1, KVW), jnp.float32)
    return pl.pallas_call(
        adam_kernel,
        in_specs=[vmem, anywhere, anywhere],
        out_specs=[vmem] * 3,
        out_shape=[row, row, jax.ShapeDtypeStruct((8, 128), jnp.bfloat16)],
        scratch_shapes=[
            pltpu.VMEM((1, KVW), jnp.float32),
            pltpu.VMEM((1, KVW), jnp.float32),
            pltpu.VMEM((8, 128), jnp.float32),
            pltpu.SemaphoreType.DMA((2,)),
        ],
        compiler_params=pltpu.CompilerParams(vmem_limit_bytes=48 * 2**20),
        cost_estimate=pl.CostEstimate(flops=2**14, bytes_accessed=2**16, transcendentals=2**10),
        name="adam",
    )(parts, first, second)


def local(normed_input, value_cotangent, basis, first_moment, second_moment):
    x_at, z_lo_at, core_at = (lax.axis_index(a) for a in ("x", "z_lo", "core"))
    swap = [(0, 1), (1, 0)]
    place = np.arange(RANK, dtype=np.int32)
    by_core = owner_row(place >> 8, place >> 4 & 15, place & 15)
    with jax.named_scope("gather_core"):
        rows = lax.dynamic_slice_in_dim(basis, (x_at >> 1) * 128 + z_lo_at * 32, 32, 0)
        rows = reorder(rows, by_core)
        low, high = rows[:, :256], rows[:, 256:]
        theirs = lax.ppermute(jnp.where(core_at == 0, high, low), "core", swap)
        chunk = jnp.where(core_at == (x_at & 1), jnp.where(core_at == 0, low, high), theirs)

    with jax.named_scope("tokens_x"):
        packed = pack(x_at, normed_input, value_cotangent, theirs)
        pieces = [packed[0]] + [
            lax.ppermute(packed[k], "x", [(i, (i + k) % 4) for i in range(4)]) for k in (1, 3, 2)
        ]
    def gather(chunk):
        with jax.named_scope("gather_z"):
            line = spread(chunk, Z, 16).reshape(512, 256)
        with jax.named_scope("gather_y"):
            return spread(line, "y", 4).reshape(QUARTER, 256)

    with jax.named_scope("gather"):
        whole = lax.cond(
            x_at < 4, gather, lambda chunk: jnp.zeros((QUARTER, 256), jnp.bfloat16),
            join([chunk], packed[1]),
        )
    with jax.named_scope("tokens_core"):
        held = join(pieces, whole)
        other_held = lax.ppermute(held, "core", swap)
    with jax.named_scope("project"):
        partial = project(other_held, whole, project(held, whole))
    with jax.named_scope("reduce_xy"):
        summed = jnp.sum(exchange(partial.reshape(16, 16, KVW), ("x", "y")), axis=0)
    with jax.named_scope("reduce_z"):
        parts = exchange(summed.reshape(16, 8, 128), Z)
    with jax.named_scope("adam"):
        new_first, new_second, normalized = adam(parts, first_moment, second_moment)
    with jax.named_scope("spread_z"):
        column = spread(normalized, Z, 16).reshape(16, KVW)
    with jax.named_scope("spread_xy"):
        own = spread(column, ("x", "y"), 16).reshape(256, KVW)
    with jax.named_scope("spread_core"):
        other = lax.ppermute(own, "core", swap)
    with jax.named_scope("decode"):
        update = decode(core_at, reorder(basis, by_core), own, other)
    return new_first, new_second, update


def solution(mesh):
    fine = Mesh(mesh.devices.reshape(4, 4, 4, 4, 2), AXES)
    weights = P(("y", "z_hi", "core"), None)
    return jax.shard_map(
        local,
        mesh=fine,
        in_specs=(P(AXES, None), P(AXES, None), weights, P(AXES, None), P(AXES, None)),
        out_specs=(P(AXES, None), P(AXES, None), weights),
        check_vma=False,
    )
```

```python
import math

import jax
import jax.numpy as jnp
import numpy as np
from jax import lax
from jax.experimental import pallas as pl
from jax.experimental.pallas import tpu as pltpu
from jax.sharding import Mesh
from jax.sharding import PartitionSpec as P

STEP = 1000

beta_first = 0.9
beta_second = 0.999
adam_epsilon = 1e-08

AXES = ("z_lo", "x", "y", "z_hi", "core")
Z = ("z_hi", "z_lo")
RANK = 512
TOKENS = 65536
KVW = 1024
QUARTER = 2048


def owner_row(core, xy, z):
    x, y = xy >> 2, xy & 3
    z_hi, z_lo = z >> 2, z & 3
    return (((z_lo * 4 + x) * 4 + y) * 4 + z_hi) * 2 + core


def reorder(basis, rows):
    pick = (lax.broadcasted_iota(jnp.int32, (RANK, RANK), 0) == rows[None, :]).astype(jnp.bfloat16)
    return jnp.dot(basis, pick, preferred_element_type=jnp.float32).astype(jnp.bfloat16)


def exchange(blocks, axes):
    return lax.all_to_all(blocks, axes, 0, 0, tiled=True)


def spread(block, axes, count):
    return exchange(jnp.broadcast_to(block[None], (count, *block.shape)), axes)


def pack_kernel(x_ref, tokens_ref, cotangent_ref, *out_refs):
    for k, out_ref in enumerate(out_refs):
        at = (x_ref[0] + k) & 3
        offset = pl.multiple_of((at & 1) * 256 + (at >> 1) * 128, 128)
        for block in range(16):
            out_ref[:, block * 128 : block * 128 + 128] = tokens_ref[
                :, pl.ds(pl.multiple_of(block * 512 + offset, 128), 128)
            ]
        out_ref[:, QUARTER:] = cotangent_ref[...]


def pack(x_at, tokens, cotangent):
    rows = 32
    return pl.pallas_call(
        pack_kernel,
        grid=(128 // rows,),
        in_specs=[
            pl.BlockSpec(memory_space=pltpu.SMEM),
            pl.BlockSpec((rows, 8192), lambda i: (i, 0)),
            pl.BlockSpec((rows, KVW), lambda i: (i, 0)),
        ],
        out_specs=[pl.BlockSpec((rows, QUARTER + KVW), lambda i: (i, 0))] * 4,
        out_shape=[jax.ShapeDtypeStruct((128, QUARTER + KVW), jnp.bfloat16)] * 4,
        compiler_params=pltpu.CompilerParams(vmem_limit_bytes=32 * 2**20),
        cost_estimate=pl.CostEstimate(flops=0, bytes_accessed=6 * 2**20, transcendentals=0),
        name="pack",
    )(x_at[None], tokens, cotangent)


def join_kernel(*refs):
    *pieces, _, out_ref = refs
    for k, piece in enumerate(pieces):
        rows = piece.shape[0]
        out_ref[k * rows : k * rows + rows] = piece[...]


def join(pieces, other):
    rows, columns = pieces[0].shape
    vmem = pl.BlockSpec(memory_space=pltpu.VMEM)
    return pl.pallas_call(
        join_kernel,
        in_specs=[vmem] * len(pieces) + [pl.BlockSpec(memory_space=pl.ANY)],
        out_specs=vmem,
        out_shape=jax.ShapeDtypeStruct((rows * len(pieces), columns), jnp.bfloat16),
        compiler_params=pltpu.CompilerParams(vmem_limit_bytes=56 * 2**20),
        cost_estimate=pl.CostEstimate(flops=0, bytes_accessed=2**20, transcendentals=0),
        name="join",
    )(*pieces, other)


def project_kernel(*refs):
    *pieces, whole_ref, out_ref, split_ref = refs
    whole = whole_ref[...]
    at, tokens = 0, split_ref.shape[0] // 2
    for piece in pieces:
        rows = piece.shape[0]
        reduced = jnp.dot(piece[:, :QUARTER], whole, preferred_element_type=jnp.float32)
        high = reduced.astype(jnp.bfloat16)
        low = (reduced - high.astype(jnp.float32)).astype(jnp.bfloat16)
        split_ref[at : at + rows] = high
        split_ref[tokens + at : tokens + at + rows] = low
        at += rows
    for n in range(0, KVW, 256):
        columns = [piece[:, QUARTER + n : QUARTER + n + 256] for piece in pieces]
        out_ref[:, n : n + 256] = lax.dot_general(
            split_ref[...],
            jnp.concatenate(columns + columns, axis=0),
            (((0,), (0,)), ((), ())),
            preferred_element_type=jnp.float32,
        )


def project(pieces, whole):
    vmem = pl.BlockSpec(memory_space=pltpu.VMEM)
    return pl.pallas_call(
        project_kernel,
        in_specs=[vmem] * (len(pieces) + 1),
        out_specs=vmem,
        out_shape=jax.ShapeDtypeStruct((256, KVW), jnp.float32),
        scratch_shapes=[pltpu.VMEM((2048, 256), jnp.bfloat16)],
        compiler_params=pltpu.CompilerParams(vmem_limit_bytes=56 * 2**20),
        cost_estimate=pl.CostEstimate(
            flops=2 * 2**30, bytes_accessed=8 * 2**20, transcendentals=0
        ),
        name="project",
    )(*pieces, whole)


def decode_kernel(core_ref, basis_ref, own_ref, other_ref, out_ref):
    total = None
    for at, rows_ref in ((core_ref[0], own_ref), (1 - core_ref[0], other_ref)):
        half = basis_ref[:, pl.ds(pl.multiple_of(at * 256, 256), 256)]
        term = jnp.dot(half, rows_ref[...], preferred_element_type=jnp.float32)
        total = term if total is None else total + term
    out_ref[...] = total.astype(jnp.bfloat16)


def decode(core_at, basis, own, other):
    vmem = pl.BlockSpec(memory_space=pltpu.VMEM)
    return pl.pallas_call(
        decode_kernel,
        in_specs=[pl.BlockSpec(memory_space=pltpu.SMEM)] + [vmem] * 3,
        out_specs=vmem,
        out_shape=jax.ShapeDtypeStruct((256, KVW), jnp.bfloat16),
        compiler_params=pltpu.CompilerParams(vmem_limit_bytes=16 * 2**20),
        cost_estimate=pl.CostEstimate(flops=2**28, bytes_accessed=2**21, transcendentals=0),
        name="decode",
    )(core_at[None], basis, own, other)


def adam_kernel(parts_ref, first_hbm, second_hbm, new_first_ref, new_second_ref, normalized_ref,
                first_ref, second_ref, step_ref, semaphores):
    fetches = [
        pltpu.make_async_copy(first_hbm, first_ref, semaphores.at[0]),
        pltpu.make_async_copy(second_hbm, second_ref, semaphores.at[1]),
    ]
    for fetch in fetches:
        fetch.start()
    shares = jnp.sum(parts_ref[...], axis=0) * (1.0 / math.sqrt(TOKENS))
    for fetch in fetches:
        fetch.wait()
    corr_first = 1.0 - beta_first**STEP
    corr_second = 1.0 - beta_second**STEP
    for n in range(8):
        columns = slice(n * 128, n * 128 + 128)
        share = shares[n : n + 1]
        new_first = beta_first * first_ref[:, columns] + (1.0 - beta_first) * share
        new_second = beta_second * second_ref[:, columns] + (1.0 - beta_second) * share * share
        new_first_ref[:, columns] = new_first
        new_second_ref[:, columns] = new_second
        step_ref[n : n + 1] = (
            new_first / corr_first / (jnp.sqrt(new_second / corr_second) + adam_epsilon)
        )
    normalized_ref[...] = step_ref[...].astype(jnp.bfloat16)


def adam(parts, first, second):
    vmem, anywhere = pl.BlockSpec(memory_space=pltpu.VMEM), pl.BlockSpec(memory_space=pl.ANY)
    row = jax.ShapeDtypeStruct((1, KVW), jnp.float32)
    return pl.pallas_call(
        adam_kernel,
        in_specs=[vmem, anywhere, anywhere],
        out_specs=[vmem] * 3,
        out_shape=[row, row, jax.ShapeDtypeStruct((8, 128), jnp.bfloat16)],
        scratch_shapes=[
            pltpu.VMEM((1, KVW), jnp.float32),
            pltpu.VMEM((1, KVW), jnp.float32),
            pltpu.VMEM((8, 128), jnp.float32),
            pltpu.SemaphoreType.DMA((2,)),
        ],
        compiler_params=pltpu.CompilerParams(vmem_limit_bytes=48 * 2**20),
        cost_estimate=pl.CostEstimate(flops=2**14, bytes_accessed=2**16, transcendentals=2**10),
        name="adam",
    )(parts, first, second)


def local(normed_input, value_cotangent, basis, first_moment, second_moment):
    x_at, z_lo_at, core_at = (lax.axis_index(a) for a in ("x", "z_lo", "core"))
    swap = [(0, 1), (1, 0)]
    place = np.arange(RANK, dtype=np.int32)
    by_core = owner_row(place >> 8, place >> 4 & 15, place & 15)
    with jax.named_scope("tokens_x"):
        packed = pack(x_at, normed_input, value_cotangent)
        pieces = [packed[0]] + [
            lax.ppermute(packed[k], "x", [(i, (i + k) % 4) for i in range(4)]) for k in (1, 3, 2)
        ]

    def gather_z(rows):
        with jax.named_scope("gather_core"):
            low, high = rows[:, :256], rows[:, 256:]
            theirs = lax.ppermute(jnp.where(core_at == 0, high, low), "core", swap)
            chunk = jnp.where(core_at == (x_at & 1), jnp.where(core_at == 0, low, high), theirs)
        with jax.named_scope("gather_z"):
            return spread(chunk, Z, 16).reshape(512, 256)

    def gather_y(line):
        with jax.named_scope("gather_y"):
            return spread(line, "y", 4).reshape(QUARTER, 256)

    def in_order(step, block, out_rows):
        return lax.cond(
            x_at < 4, step, lambda block: jnp.zeros((out_rows, 256), jnp.bfloat16), block
        )

    with jax.named_scope("gather"):
        rows = lax.dynamic_slice_in_dim(basis, (x_at >> 1) * 128 + z_lo_at * 32, 32, 0)
        rows = reorder(rows, by_core)
        line = in_order(gather_z, join([rows], packed[1]), 512)
    with jax.named_scope("tokens_core"):
        held = join(pieces, line)
        other_held = lax.ppermute(held, "core", swap)
    with jax.named_scope("gather"):
        whole = in_order(gather_y, join([line], held), QUARTER)
    with jax.named_scope("project"):
        partial = project([held, other_held], whole)
    with jax.named_scope("reduce_xy"):
        summed = jnp.sum(exchange(partial.reshape(16, 16, KVW), ("x", "y")), axis=0)
    with jax.named_scope("reduce_z"):
        parts = exchange(summed.reshape(16, 8, 128), Z)
    with jax.named_scope("adam"):
        new_first, new_second, normalized = adam(parts, first_moment, second_moment)
    with jax.named_scope("spread_z"):
        column = spread(normalized, Z, 16).reshape(16, KVW)
    with jax.named_scope("spread_xy"):
        own = spread(column, ("x", "y"), 16).reshape(256, KVW)
    with jax.named_scope("spread_core"):
        other = lax.ppermute(own, "core", swap)
    with jax.named_scope("decode"):
        update = decode(core_at, reorder(basis, by_core), own, other)
    return new_first, new_second, update


def solution(mesh):
    fine = Mesh(mesh.devices.reshape(4, 4, 4, 4, 2), AXES)
    weights = P(("y", "z_hi", "core"), None)
    return jax.shard_map(
        local,
        mesh=fine,
        in_specs=(P(AXES, None), P(AXES, None), weights, P(AXES, None), P(AXES, None)),
        out_specs=(P(AXES, None), P(AXES, None), weights),
        check_vma=False,
    )
```

```python
import math

import jax
import jax.numpy as jnp
import numpy as np
from jax import lax
from jax.experimental import pallas as pl
from jax.experimental.pallas import tpu as pltpu
from jax.sharding import Mesh
from jax.sharding import PartitionSpec as P

STEP = 1000

beta_first = 0.9
beta_second = 0.999
adam_epsilon = 1e-08

AXES = ("z_lo", "x", "y", "z_hi", "core")
Z = ("z_hi", "z_lo")
RANK = 512
TOKENS = 65536
KVW = 1024
QUARTER = 2048


def owner_row(core, xy, z):
    x, y = xy >> 2, xy & 3
    z_hi, z_lo = z >> 2, z & 3
    return (((z_lo * 4 + x) * 4 + y) * 4 + z_hi) * 2 + core


def reorder(basis, rows):
    pick = (lax.broadcasted_iota(jnp.int32, (RANK, RANK), 0) == rows[None, :]).astype(jnp.bfloat16)
    return jnp.dot(basis, pick, preferred_element_type=jnp.float32).astype(jnp.bfloat16)


def exchange(blocks, axes):
    return lax.all_to_all(blocks, axes, 0, 0, tiled=True)


def spread(block, axes, count):
    return exchange(jnp.broadcast_to(block[None], (count, *block.shape)), axes)


def pack_kernel(x_ref, tokens_ref, cotangent_ref, *out_refs):
    for k, out_ref in enumerate(out_refs):
        at = (x_ref[0] + k) & 3
        offset = pl.multiple_of((at & 1) * 256 + (at >> 1) * 128, 128)
        for block in range(16):
            out_ref[:, block * 128 : block * 128 + 128] = tokens_ref[
                :, pl.ds(pl.multiple_of(block * 512 + offset, 128), 128)
            ]
        out_ref[:, QUARTER:] = cotangent_ref[...]


def pack(x_at, tokens, cotangent):
    rows = 32
    return pl.pallas_call(
        pack_kernel,
        grid=(128 // rows,),
        in_specs=[
            pl.BlockSpec(memory_space=pltpu.SMEM),
            pl.BlockSpec((rows, 8192), lambda i: (i, 0)),
            pl.BlockSpec((rows, KVW), lambda i: (i, 0)),
        ],
        out_specs=[pl.BlockSpec((rows, QUARTER + KVW), lambda i: (i, 0))] * 4,
        out_shape=[jax.ShapeDtypeStruct((128, QUARTER + KVW), jnp.bfloat16)] * 4,
        compiler_params=pltpu.CompilerParams(vmem_limit_bytes=32 * 2**20),
        cost_estimate=pl.CostEstimate(flops=0, bytes_accessed=6 * 2**20, transcendentals=0),
        name="pack",
    )(x_at[None], tokens, cotangent)


def join_kernel(*refs):
    *pieces, _, out_ref = refs
    for k, piece in enumerate(pieces):
        rows = piece.shape[0]
        out_ref[k * rows : k * rows + rows] = piece[...]


def join(pieces, other):
    rows, columns = pieces[0].shape
    vmem = pl.BlockSpec(memory_space=pltpu.VMEM)
    return pl.pallas_call(
        join_kernel,
        in_specs=[vmem] * len(pieces) + [pl.BlockSpec(memory_space=pl.ANY)],
        out_specs=vmem,
        out_shape=jax.ShapeDtypeStruct((rows * len(pieces), columns), jnp.bfloat16),
        compiler_params=pltpu.CompilerParams(vmem_limit_bytes=16 * 2**20),
        cost_estimate=pl.CostEstimate(flops=0, bytes_accessed=2**20, transcendentals=0),
        name="join",
    )(*pieces, other)


def project_kernel(*refs):
    *pieces, whole_ref, out_ref, split_ref = refs
    whole = whole_ref[...]
    at, tokens = 0, split_ref.shape[0] // 2
    for piece in pieces:
        rows = piece.shape[0]
        reduced = jnp.dot(piece[:, :QUARTER], whole, preferred_element_type=jnp.float32)
        high = reduced.astype(jnp.bfloat16)
        low = (reduced - high.astype(jnp.float32)).astype(jnp.bfloat16)
        split_ref[at : at + rows] = high
        split_ref[tokens + at : tokens + at + rows] = low
        at += rows
    for n in range(0, KVW, 256):
        columns = [piece[:, QUARTER + n : QUARTER + n + 256] for piece in pieces]
        out_ref[:, n : n + 256] = lax.dot_general(
            split_ref[...],
            jnp.concatenate(columns + columns, axis=0),
            (((0,), (0,)), ((), ())),
            preferred_element_type=jnp.float32,
        )


def project(pieces, whole):
    vmem = pl.BlockSpec(memory_space=pltpu.VMEM)
    return pl.pallas_call(
        project_kernel,
        in_specs=[vmem] * (len(pieces) + 1),
        out_specs=vmem,
        out_shape=jax.ShapeDtypeStruct((256, KVW), jnp.float32),
        scratch_shapes=[pltpu.VMEM((2048, 256), jnp.bfloat16)],
        compiler_params=pltpu.CompilerParams(vmem_limit_bytes=40 * 2**20),
        cost_estimate=pl.CostEstimate(
            flops=2 * 2**30, bytes_accessed=8 * 2**20, transcendentals=0
        ),
        name="project",
    )(*pieces, whole)


def decode_kernel(core_ref, basis_ref, own_ref, other_ref, out_ref):
    total = None
    for at, rows_ref in ((core_ref[0], own_ref), (1 - core_ref[0], other_ref)):
        half = basis_ref[:, pl.ds(pl.multiple_of(at * 256, 256), 256)]
        term = jnp.dot(half, rows_ref[...], preferred_element_type=jnp.float32)
        total = term if total is None else total + term
    out_ref[...] = total.astype(jnp.bfloat16)


def decode(core_at, basis, own, other):
    vmem = pl.BlockSpec(memory_space=pltpu.VMEM)
    return pl.pallas_call(
        decode_kernel,
        in_specs=[pl.BlockSpec(memory_space=pltpu.SMEM)] + [vmem] * 3,
        out_specs=vmem,
        out_shape=jax.ShapeDtypeStruct((256, KVW), jnp.bfloat16),
        compiler_params=pltpu.CompilerParams(vmem_limit_bytes=16 * 2**20),
        cost_estimate=pl.CostEstimate(flops=2**28, bytes_accessed=2**21, transcendentals=0),
        name="decode",
    )(core_at[None], basis, own, other)


def adam_kernel(parts_ref, first_hbm, second_hbm, new_first_ref, new_second_ref, normalized_ref,
                first_ref, second_ref, step_ref, semaphores):
    fetches = [
        pltpu.make_async_copy(first_hbm, first_ref, semaphores.at[0]),
        pltpu.make_async_copy(second_hbm, second_ref, semaphores.at[1]),
    ]
    for fetch in fetches:
        fetch.start()
    shares = jnp.sum(parts_ref[...], axis=0) * (1.0 / math.sqrt(TOKENS))
    for fetch in fetches:
        fetch.wait()
    corr_first = 1.0 - beta_first**STEP
    corr_second = 1.0 - beta_second**STEP
    for n in range(8):
        columns = slice(n * 128, n * 128 + 128)
        share = shares[n : n + 1]
        new_first = beta_first * first_ref[:, columns] + (1.0 - beta_first) * share
        new_second = beta_second * second_ref[:, columns] + (1.0 - beta_second) * share * share
        new_first_ref[:, columns] = new_first
        new_second_ref[:, columns] = new_second
        step_ref[n : n + 1] = (
            new_first / corr_first / (jnp.sqrt(new_second / corr_second) + adam_epsilon)
        )
    normalized_ref[...] = step_ref[...].astype(jnp.bfloat16)


def adam(parts, first, second):
    vmem, anywhere = pl.BlockSpec(memory_space=pltpu.VMEM), pl.BlockSpec(memory_space=pl.ANY)
    row = jax.ShapeDtypeStruct((1, KVW), jnp.float32)
    return pl.pallas_call(
        adam_kernel,
        in_specs=[vmem, anywhere, anywhere],
        out_specs=[vmem] * 3,
        out_shape=[row, row, jax.ShapeDtypeStruct((8, 128), jnp.bfloat16)],
        scratch_shapes=[
            pltpu.VMEM((1, KVW), jnp.float32),
            pltpu.VMEM((1, KVW), jnp.float32),
            pltpu.VMEM((8, 128), jnp.float32),
            pltpu.SemaphoreType.DMA((2,)),
        ],
        compiler_params=pltpu.CompilerParams(vmem_limit_bytes=48 * 2**20),
        cost_estimate=pl.CostEstimate(flops=2**14, bytes_accessed=2**16, transcendentals=2**10),
        name="adam",
    )(parts, first, second)


def local(normed_input, value_cotangent, basis, first_moment, second_moment):
    x_at, z_lo_at, core_at = (lax.axis_index(a) for a in ("x", "z_lo", "core"))
    swap = [(0, 1), (1, 0)]
    place = np.arange(RANK, dtype=np.int32)
    by_core = owner_row(place >> 8, place >> 4 & 15, place & 15)
    with jax.named_scope("tokens_x"):
        packed = pack(x_at, normed_input, value_cotangent)
        pieces = [packed[0]] + [
            lax.ppermute(packed[k], "x", [(i, (i + k) % 4) for i in range(4)]) for k in (1, 3, 2)
        ]
    def gather(rows):
        with jax.named_scope("gather_core"):
            low, high = rows[:, :256], rows[:, 256:]
            theirs = lax.ppermute(jnp.where(core_at == 0, high, low), "core", swap)
            chunk = jnp.where(core_at == (x_at & 1), jnp.where(core_at == 0, low, high), theirs)
        with jax.named_scope("gather_z"):
            line = spread(chunk, Z, 16).reshape(512, 256)
        with jax.named_scope("gather_y"):
            return spread(line, "y", 4).reshape(QUARTER, 256)

    with jax.named_scope("gather"):
        rows = lax.dynamic_slice_in_dim(basis, (x_at >> 1) * 128 + z_lo_at * 32, 32, 0)
        rows = reorder(rows, by_core)
        whole = lax.cond(
            x_at < 4, gather, lambda rows: jnp.zeros((QUARTER, 256), jnp.bfloat16),
            join([rows], packed[1]),
        )
    with jax.named_scope("tokens_core"):
        held = join(pieces, whole)
        held = [held, lax.ppermute(held, "core", swap)]
    with jax.named_scope("project"):
        partial = project(held, whole)
    with jax.named_scope("reduce_xy"):
        summed = jnp.sum(exchange(partial.reshape(16, 16, KVW), ("x", "y")), axis=0)
    with jax.named_scope("reduce_z"):
        parts = exchange(summed.reshape(16, 8, 128), Z)
    with jax.named_scope("adam"):
        new_first, new_second, normalized = adam(parts, first_moment, second_moment)
    with jax.named_scope("spread_z"):
        column = spread(normalized, Z, 16).reshape(16, KVW)
    with jax.named_scope("spread_xy"):
        own = spread(column, ("x", "y"), 16).reshape(256, KVW)
    with jax.named_scope("spread_core"):
        other = lax.ppermute(own, "core", swap)
    with jax.named_scope("decode"):
        update = decode(core_at, reorder(basis, by_core), own, other)
    return new_first, new_second, update


def solution(mesh):
    fine = Mesh(mesh.devices.reshape(4, 4, 4, 4, 2), AXES)
    weights = P(("y", "z_hi", "core"), None)
    return jax.shard_map(
        local,
        mesh=fine,
        in_specs=(P(AXES, None), P(AXES, None), weights, P(AXES, None), P(AXES, None)),
        out_specs=(P(AXES, None), P(AXES, None), weights),
        check_vma=False,
    )
```

```python
import math

import jax
import jax.numpy as jnp
import numpy as np
from jax import lax
from jax.experimental import pallas as pl
from jax.experimental.pallas import tpu as pltpu
from jax.sharding import Mesh
from jax.sharding import PartitionSpec as P

STEP = 1000

beta_first = 0.9
beta_second = 0.999
adam_epsilon = 1e-08

AXES = ("z_lo", "x", "y", "z_hi", "core")
Z = ("z_hi", "z_lo")
RANK = 512
TOKENS = 65536
KVW = 1024
QUARTER = 2048


def owner_row(core, xy, z):
    x, y = xy >> 2, xy & 3
    z_hi, z_lo = z >> 2, z & 3
    return (((z_lo * 4 + x) * 4 + y) * 4 + z_hi) * 2 + core


def reorder(basis, rows):
    pick = (lax.broadcasted_iota(jnp.int32, (RANK, RANK), 0) == rows[None, :]).astype(jnp.bfloat16)
    return jnp.dot(basis, pick, preferred_element_type=jnp.float32).astype(jnp.bfloat16)


def exchange(blocks, axes):
    return lax.all_to_all(blocks, axes, 0, 0, tiled=True)


def spread(block, axes, count):
    return exchange(jnp.broadcast_to(block[None], (count, *block.shape)), axes)


def pack_kernel(x_ref, tokens_ref, cotangent_ref, *out_refs):
    for k, out_ref in enumerate(out_refs):
        at = (x_ref[0] + k) & 3
        offset = pl.multiple_of((at & 1) * 256 + (at >> 1) * 128, 128)
        for block in range(16):
            out_ref[:, block * 128 : block * 128 + 128] = tokens_ref[
                :, pl.ds(pl.multiple_of(block * 512 + offset, 128), 128)
            ]
        out_ref[:, QUARTER:] = cotangent_ref[...]


def pack(x_at, tokens, cotangent):
    rows = 32
    return pl.pallas_call(
        pack_kernel,
        grid=(128 // rows,),
        in_specs=[
            pl.BlockSpec(memory_space=pltpu.SMEM),
            pl.BlockSpec((rows, 8192), lambda i: (i, 0)),
            pl.BlockSpec((rows, KVW), lambda i: (i, 0)),
        ],
        out_specs=[pl.BlockSpec((rows, QUARTER + KVW), lambda i: (i, 0))] * 4,
        out_shape=[jax.ShapeDtypeStruct((128, QUARTER + KVW), jnp.bfloat16)] * 4,
        compiler_params=pltpu.CompilerParams(vmem_limit_bytes=32 * 2**20),
        cost_estimate=pl.CostEstimate(flops=0, bytes_accessed=6 * 2**20, transcendentals=0),
        name="pack",
    )(x_at[None], tokens, cotangent)


def join_kernel(*refs):
    *pieces, _, out_ref = refs
    for k, piece in enumerate(pieces):
        rows = piece.shape[0]
        out_ref[k * rows : k * rows + rows] = piece[...]


def join(pieces, other):
    rows, columns = pieces[0].shape
    vmem = pl.BlockSpec(memory_space=pltpu.VMEM)
    return pl.pallas_call(
        join_kernel,
        in_specs=[vmem] * len(pieces) + [pl.BlockSpec(memory_space=pl.ANY)],
        out_specs=vmem,
        out_shape=jax.ShapeDtypeStruct((rows * len(pieces), columns), jnp.bfloat16),
        compiler_params=pltpu.CompilerParams(vmem_limit_bytes=16 * 2**20),
        cost_estimate=pl.CostEstimate(flops=0, bytes_accessed=2**20, transcendentals=0),
        name="join",
    )(*pieces, other)


def project_kernel(*refs):
    *pieces, whole_ref, out_ref, split_ref, sum_ref = refs
    whole = whole_ref[...]
    at, tokens = 0, split_ref.shape[0] // 2
    for piece in pieces:
        rows = piece.shape[0]
        reduced = jnp.dot(piece[:, :QUARTER], whole, preferred_element_type=jnp.float32)
        high = reduced.astype(jnp.bfloat16)
        low = (reduced - high.astype(jnp.float32)).astype(jnp.bfloat16)
        split_ref[at : at + rows] = high
        split_ref[tokens + at : tokens + at + rows] = low
        at += rows
    for n in range(0, KVW, 256):
        columns = [piece[:, QUARTER + n : QUARTER + n + 256] for piece in pieces]
        sum_ref[:, n : n + 256] = lax.dot_general(
            split_ref[...],
            jnp.concatenate(columns + columns, axis=0),
            (((0,), (0,)), ((), ())),
            preferred_element_type=jnp.float32,
        )
    top = jnp.max(jnp.abs(sum_ref[...]), axis=1, keepdims=True)
    exponent = jnp.ceil(jnp.log2(jnp.maximum(top, 1e-36))) + 1.0
    exponent = jnp.broadcast_to(exponent, (256, 128))
    scale = jnp.exp2(-exponent)
    out_ref[:, 8] = exponent.reshape(16, 16, 128)
    for n in range(8):
        out_ref[:, n] = (sum_ref[:, n * 128 : n * 128 + 128] * scale).reshape(16, 16, 128)


def project(pieces, whole):
    vmem = pl.BlockSpec(memory_space=pltpu.VMEM)
    return pl.pallas_call(
        project_kernel,
        in_specs=[vmem] * (len(pieces) + 1),
        out_specs=vmem,
        out_shape=jax.ShapeDtypeStruct((16, 9, 16, 128), jnp.float32),
        scratch_shapes=[
            pltpu.VMEM((2048, 256), jnp.bfloat16),
            pltpu.VMEM((256, KVW), jnp.float32),
        ],
        compiler_params=pltpu.CompilerParams(vmem_limit_bytes=40 * 2**20),
        cost_estimate=pl.CostEstimate(
            flops=2 * 2**30, bytes_accessed=8 * 2**20, transcendentals=0
        ),
        name="project",
    )(*pieces, whole)


def decode_kernel(core_ref, basis_ref, own_ref, other_ref, out_ref):
    total = None
    for at, rows_ref in ((core_ref[0], own_ref), (1 - core_ref[0], other_ref)):
        half = basis_ref[:, pl.ds(pl.multiple_of(at * 256, 256), 256)]
        term = jnp.dot(half, rows_ref[...], preferred_element_type=jnp.float32)
        total = term if total is None else total + term
    out_ref[...] = total.astype(jnp.bfloat16)


def decode(core_at, basis, own, other):
    vmem = pl.BlockSpec(memory_space=pltpu.VMEM)
    return pl.pallas_call(
        decode_kernel,
        in_specs=[pl.BlockSpec(memory_space=pltpu.SMEM)] + [vmem] * 3,
        out_specs=vmem,
        out_shape=jax.ShapeDtypeStruct((256, KVW), jnp.bfloat16),
        compiler_params=pltpu.CompilerParams(vmem_limit_bytes=16 * 2**20),
        cost_estimate=pl.CostEstimate(flops=2**28, bytes_accessed=2**21, transcendentals=0),
        name="decode",
    )(core_at[None], basis, own, other)


def adam_kernel(parts_ref, first_hbm, second_hbm, new_first_ref, new_second_ref, normalized_ref,
                first_ref, second_ref, step_ref, semaphores):
    fetches = [
        pltpu.make_async_copy(first_hbm, first_ref, semaphores.at[0]),
        pltpu.make_async_copy(second_hbm, second_ref, semaphores.at[1]),
    ]
    for fetch in fetches:
        fetch.start()
    shares = jnp.sum(parts_ref[...], axis=0) * (1.0 / math.sqrt(TOKENS))
    for fetch in fetches:
        fetch.wait()
    corr_first = 1.0 - beta_first**STEP
    corr_second = 1.0 - beta_second**STEP
    for n in range(8):
        columns = slice(n * 128, n * 128 + 128)
        share = shares[n : n + 1]
        new_first = beta_first * first_ref[:, columns] + (1.0 - beta_first) * share
        new_second = beta_second * second_ref[:, columns] + (1.0 - beta_second) * share * share
        new_first_ref[:, columns] = new_first
        new_second_ref[:, columns] = new_second
        step_ref[n : n + 1] = (
            new_first / corr_first / (jnp.sqrt(new_second / corr_second) + adam_epsilon)
        )
    normalized_ref[...] = step_ref[...].astype(jnp.bfloat16)


def adam(parts, first, second):
    vmem, anywhere = pl.BlockSpec(memory_space=pltpu.VMEM), pl.BlockSpec(memory_space=pl.ANY)
    row = jax.ShapeDtypeStruct((1, KVW), jnp.float32)
    return pl.pallas_call(
        adam_kernel,
        in_specs=[vmem, anywhere, anywhere],
        out_specs=[vmem] * 3,
        out_shape=[row, row, jax.ShapeDtypeStruct((8, 128), jnp.bfloat16)],
        scratch_shapes=[
            pltpu.VMEM((1, KVW), jnp.float32),
            pltpu.VMEM((1, KVW), jnp.float32),
            pltpu.VMEM((8, 128), jnp.float32),
            pltpu.SemaphoreType.DMA((2,)),
        ],
        compiler_params=pltpu.CompilerParams(vmem_limit_bytes=48 * 2**20),
        cost_estimate=pl.CostEstimate(flops=2**14, bytes_accessed=2**16, transcendentals=2**10),
        name="adam",
    )(parts, first, second)


def local(normed_input, value_cotangent, basis, first_moment, second_moment):
    x_at, z_lo_at, core_at = (lax.axis_index(a) for a in ("x", "z_lo", "core"))
    swap = [(0, 1), (1, 0)]
    place = np.arange(RANK, dtype=np.int32)
    by_core = owner_row(place >> 8, place >> 4 & 15, place & 15)
    with jax.named_scope("tokens_x"):
        packed = pack(x_at, normed_input, value_cotangent)
        pieces = [packed[0]] + [
            lax.ppermute(packed[k], "x", [(i, (i + k) % 4) for i in range(4)]) for k in (1, 3, 2)
        ]
    def gather(rows):
        with jax.named_scope("gather_core"):
            low, high = rows[:, :256], rows[:, 256:]
            theirs = lax.ppermute(jnp.where(core_at == 0, high, low), "core", swap)
            chunk = jnp.where(core_at == (x_at & 1), jnp.where(core_at == 0, low, high), theirs)
        with jax.named_scope("gather_z"):
            line = spread(chunk, Z, 16).reshape(512, 256)
        with jax.named_scope("gather_y"):
            return spread(line, "y", 4).reshape(QUARTER, 256)

    with jax.named_scope("gather"):
        rows = lax.dynamic_slice_in_dim(basis, (x_at >> 1) * 128 + z_lo_at * 32, 32, 0)
        rows = reorder(rows, by_core)
        whole = lax.cond(
            x_at < 4, gather, lambda rows: jnp.zeros((QUARTER, 256), jnp.bfloat16),
            join([rows], packed[1]),
        )
    with jax.named_scope("tokens_core"):
        held = join(pieces, whole)
        held = [held, lax.ppermute(held, "core", swap)]
    with jax.named_scope("project"):
        partial = project(held, whole)
    with jax.named_scope("reduce_xy"):
        parts = exchange(partial.astype(jnp.float16), ("x", "y")).astype(jnp.float32)
        summed = jnp.sum(parts[:, :8] * jnp.exp2(parts[:, 8:]), axis=0).transpose(1, 0, 2)
    with jax.named_scope("reduce_z"):
        parts = exchange(summed, Z)
    with jax.named_scope("adam"):
        new_first, new_second, normalized = adam(parts, first_moment, second_moment)
    with jax.named_scope("spread_z"):
        column = spread(normalized, Z, 16).reshape(16, KVW)
    with jax.named_scope("spread_xy"):
        own = spread(column, ("x", "y"), 16).reshape(256, KVW)
    with jax.named_scope("spread_core"):
        other = lax.ppermute(own, "core", swap)
    with jax.named_scope("decode"):
        update = decode(core_at, reorder(basis, by_core), own, other)
    return new_first, new_second, update


def solution(mesh):
    fine = Mesh(mesh.devices.reshape(4, 4, 4, 4, 2), AXES)
    weights = P(("y", "z_hi", "core"), None)
    return jax.shard_map(
        local,
        mesh=fine,
        in_specs=(P(AXES, None), P(AXES, None), weights, P(AXES, None), P(AXES, None)),
        out_specs=(P(AXES, None), P(AXES, None), weights),
        check_vma=False,
    )
```

```python
import math

import jax
import jax.numpy as jnp
import numpy as np
from jax import lax
from jax.experimental import pallas as pl
from jax.experimental.pallas import tpu as pltpu
from jax.sharding import Mesh
from jax.sharding import PartitionSpec as P

STEP = 1000

beta_first = 0.9
beta_second = 0.999
adam_epsilon = 1e-08

AXES = ("z_lo", "x", "y", "z_hi", "core")
Z = ("z_hi", "z_lo")
RANK = 512
TOKENS = 65536
KVW = 1024
QUARTER = 2048


def owner_row(core, xy, z):
    x, y = xy >> 2, xy & 3
    z_hi, z_lo = z >> 2, z & 3
    return (((z_lo * 4 + x) * 4 + y) * 4 + z_hi) * 2 + core


def reorder(basis, rows):
    pick = (lax.broadcasted_iota(jnp.int32, (RANK, RANK), 0) == rows[None, :]).astype(jnp.bfloat16)
    return jnp.dot(basis, pick, preferred_element_type=jnp.float32).astype(jnp.bfloat16)


def exchange(blocks, axes):
    return lax.all_to_all(blocks, axes, 0, 0, tiled=True)


def spread(block, axes, count):
    return exchange(jnp.broadcast_to(block[None], (count, *block.shape)), axes)


def pack_kernel(x_ref, tokens_ref, cotangent_ref, *out_refs):
    for k, out_ref in enumerate(out_refs):
        at = (x_ref[0] + k) & 3
        offset = pl.multiple_of((at & 1) * 256 + (at >> 1) * 128, 128)
        for block in range(16):
            out_ref[:, block * 128 : block * 128 + 128] = tokens_ref[
                :, pl.ds(pl.multiple_of(block * 512 + offset, 128), 128)
            ]
        out_ref[:, QUARTER:] = cotangent_ref[...]


def pack(x_at, tokens, cotangent):
    rows = 32
    return pl.pallas_call(
        pack_kernel,
        grid=(128 // rows,),
        in_specs=[
            pl.BlockSpec(memory_space=pltpu.SMEM),
            pl.BlockSpec((rows, 8192), lambda i: (i, 0)),
            pl.BlockSpec((rows, KVW), lambda i: (i, 0)),
        ],
        out_specs=[pl.BlockSpec((rows, QUARTER + KVW), lambda i: (i, 0))] * 4,
        out_shape=[jax.ShapeDtypeStruct((128, QUARTER + KVW), jnp.bfloat16)] * 4,
        compiler_params=pltpu.CompilerParams(vmem_limit_bytes=32 * 2**20),
        cost_estimate=pl.CostEstimate(flops=0, bytes_accessed=6 * 2**20, transcendentals=0),
        name="pack",
    )(x_at[None], tokens, cotangent)


def join_kernel(*refs):
    *pieces, _, out_ref = refs
    for k, piece in enumerate(pieces):
        rows = piece.shape[0]
        out_ref[k * rows : k * rows + rows] = piece[...]


def join(pieces, other):
    rows, columns = pieces[0].shape
    vmem = pl.BlockSpec(memory_space=pltpu.VMEM)
    return pl.pallas_call(
        join_kernel,
        in_specs=[vmem] * len(pieces) + [pl.BlockSpec(memory_space=pl.ANY)],
        out_specs=vmem,
        out_shape=jax.ShapeDtypeStruct((rows * len(pieces), columns), jnp.bfloat16),
        compiler_params=pltpu.CompilerParams(vmem_limit_bytes=16 * 2**20),
        cost_estimate=pl.CostEstimate(flops=0, bytes_accessed=2**20, transcendentals=0),
        name="join",
    )(*pieces, other)


def project_kernel(*refs):
    *pieces, whole_ref, out_ref, split_ref, sum_ref = refs
    whole = whole_ref[...]
    at, tokens = 0, split_ref.shape[0] // 2
    for piece in pieces:
        rows = piece.shape[0]
        reduced = jnp.dot(piece[:, :QUARTER], whole, preferred_element_type=jnp.float32)
        high = reduced.astype(jnp.bfloat16)
        low = (reduced - high.astype(jnp.float32)).astype(jnp.bfloat16)
        split_ref[at : at + rows] = high
        split_ref[tokens + at : tokens + at + rows] = low
        at += rows
    for n in range(0, KVW, 256):
        columns = [piece[:, QUARTER + n : QUARTER + n + 256] for piece in pieces]
        sum_ref[:, n : n + 256] = lax.dot_general(
            split_ref[...],
            jnp.concatenate(columns + columns, axis=0),
            (((0,), (0,)), ((), ())),
            preferred_element_type=jnp.float32,
        )
    top = jnp.max(jnp.abs(sum_ref[...]), axis=1, keepdims=True)
    exponent = jnp.ceil(jnp.log2(jnp.maximum(top, 1e-36))) + 1.0
    exponent = jnp.broadcast_to(exponent, (256, 128))
    scale = jnp.exp2(-exponent)
    out_ref[:, 8] = exponent.reshape(16, 16, 128)
    for n in range(8):
        out_ref[:, n] = (sum_ref[:, n * 128 : n * 128 + 128] * scale).reshape(16, 16, 128)


def project(pieces, whole):
    vmem = pl.BlockSpec(memory_space=pltpu.VMEM)
    return pl.pallas_call(
        project_kernel,
        in_specs=[vmem] * (len(pieces) + 1),
        out_specs=vmem,
        out_shape=jax.ShapeDtypeStruct((16, 9, 16, 128), jnp.float32),
        scratch_shapes=[
            pltpu.VMEM((2048, 256), jnp.bfloat16),
            pltpu.VMEM((256, KVW), jnp.float32),
        ],
        compiler_params=pltpu.CompilerParams(vmem_limit_bytes=40 * 2**20),
        cost_estimate=pl.CostEstimate(
            flops=2 * 2**30, bytes_accessed=8 * 2**20, transcendentals=0
        ),
        name="project",
    )(*pieces, whole)


def decode_kernel(core_ref, basis_ref, own_ref, other_ref, out_ref):
    total = None
    for at, rows_ref in ((core_ref[0], own_ref), (1 - core_ref[0], other_ref)):
        half = basis_ref[:, pl.ds(pl.multiple_of(at * 256, 256), 256)]
        term = jnp.dot(half, rows_ref[...], preferred_element_type=jnp.float32)
        total = term if total is None else total + term
    out_ref[...] = total.astype(jnp.bfloat16)


def decode(core_at, basis, own, other):
    vmem = pl.BlockSpec(memory_space=pltpu.VMEM)
    return pl.pallas_call(
        decode_kernel,
        in_specs=[pl.BlockSpec(memory_space=pltpu.SMEM)] + [vmem] * 3,
        out_specs=vmem,
        out_shape=jax.ShapeDtypeStruct((256, KVW), jnp.bfloat16),
        compiler_params=pltpu.CompilerParams(vmem_limit_bytes=16 * 2**20),
        cost_estimate=pl.CostEstimate(flops=2**28, bytes_accessed=2**21, transcendentals=0),
        name="decode",
    )(core_at[None], basis, own, other)


def adam_kernel(parts_ref, first_hbm, second_hbm, new_first_ref, new_second_ref, normalized_ref,
                first_ref, second_ref, step_ref, semaphores):
    fetches = [
        pltpu.make_async_copy(first_hbm, first_ref, semaphores.at[0]),
        pltpu.make_async_copy(second_hbm, second_ref, semaphores.at[1]),
    ]
    for fetch in fetches:
        fetch.start()
    shares = jnp.sum(parts_ref[...], axis=0) * (1.0 / math.sqrt(TOKENS))
    for fetch in fetches:
        fetch.wait()
    corr_first = 1.0 - beta_first**STEP
    corr_second = 1.0 - beta_second**STEP
    for n in range(8):
        columns = slice(n * 128, n * 128 + 128)
        share = shares[n : n + 1]
        new_first = beta_first * first_ref[:, columns] + (1.0 - beta_first) * share
        new_second = beta_second * second_ref[:, columns] + (1.0 - beta_second) * share * share
        new_first_ref[:, columns] = new_first
        new_second_ref[:, columns] = new_second
        step_ref[n : n + 1] = (
            new_first / corr_first / (jnp.sqrt(new_second / corr_second) + adam_epsilon)
        )
    normalized_ref[...] = step_ref[...].astype(jnp.bfloat16)


def adam(parts, first, second):
    vmem, anywhere = pl.BlockSpec(memory_space=pltpu.VMEM), pl.BlockSpec(memory_space=pl.ANY)
    row = jax.ShapeDtypeStruct((1, KVW), jnp.float32)
    return pl.pallas_call(
        adam_kernel,
        in_specs=[vmem, anywhere, anywhere],
        out_specs=[vmem] * 3,
        out_shape=[row, row, jax.ShapeDtypeStruct((8, 128), jnp.bfloat16)],
        scratch_shapes=[
            pltpu.VMEM((1, KVW), jnp.float32),
            pltpu.VMEM((1, KVW), jnp.float32),
            pltpu.VMEM((8, 128), jnp.float32),
            pltpu.SemaphoreType.DMA((2,)),
        ],
        compiler_params=pltpu.CompilerParams(vmem_limit_bytes=48 * 2**20),
        cost_estimate=pl.CostEstimate(flops=2**14, bytes_accessed=2**16, transcendentals=2**10),
        name="adam",
    )(parts, first, second)


def local(normed_input, value_cotangent, basis, first_moment, second_moment):
    x_at, z_lo_at, core_at = (lax.axis_index(a) for a in ("x", "z_lo", "core"))
    swap = [(0, 1), (1, 0)]
    place = np.arange(RANK, dtype=np.int32)
    by_core = owner_row(place >> 8, place >> 4 & 15, place & 15)
    with jax.named_scope("tokens_x"):
        packed = pack(x_at, normed_input, value_cotangent)
        pieces = [packed[0]] + [
            lax.ppermute(packed[k], "x", [(i, (i + k) % 4) for i in range(4)]) for k in (1, 3, 2)
        ]
    def gather(rows):
        with jax.named_scope("gather_core"):
            low, high = rows[:, :256], rows[:, 256:]
            theirs = lax.ppermute(jnp.where(core_at == 0, high, low), "core", swap)
            chunk = jnp.where(core_at == (x_at & 1), jnp.where(core_at == 0, low, high), theirs)
        with jax.named_scope("gather_z"):
            return spread(chunk, Z, 16).reshape(512, 256)

    with jax.named_scope("gather"):
        rows = lax.dynamic_slice_in_dim(basis, (x_at >> 1) * 128 + z_lo_at * 32, 32, 0)
        rows = reorder(rows, by_core)
        line = lax.cond(
            x_at < 4, gather, lambda rows: jnp.zeros((512, 256), jnp.bfloat16),
            join([rows], packed[1]),
        )
    with jax.named_scope("gather_y"):
        whole = spread(line, "y", 4).reshape(QUARTER, 256)
    with jax.named_scope("tokens_core"):
        held = join(pieces, line)
        held = [held, lax.ppermute(held, "core", swap)]
    with jax.named_scope("project"):
        partial = project(held, whole)
    with jax.named_scope("reduce_xy"):
        parts = exchange(partial.astype(jnp.float16), ("x", "y")).astype(jnp.float32)
        summed = jnp.sum(parts[:, :8] * jnp.exp2(parts[:, 8:]), axis=0).transpose(1, 0, 2)
    with jax.named_scope("reduce_z"):
        parts = exchange(summed, Z)
    with jax.named_scope("adam"):
        new_first, new_second, normalized = adam(parts, first_moment, second_moment)
    with jax.named_scope("spread_z"):
        column = spread(normalized, Z, 16).reshape(16, KVW)
    with jax.named_scope("spread_xy"):
        own = spread(column, ("x", "y"), 16).reshape(256, KVW)
    with jax.named_scope("spread_core"):
        other = lax.ppermute(own, "core", swap)
    with jax.named_scope("decode"):
        update = decode(core_at, reorder(basis, by_core), own, other)
    return new_first, new_second, update


def solution(mesh):
    fine = Mesh(mesh.devices.reshape(4, 4, 4, 4, 2), AXES)
    weights = P(("y", "z_hi", "core"), None)
    return jax.shard_map(
        local,
        mesh=fine,
        in_specs=(P(AXES, None), P(AXES, None), weights, P(AXES, None), P(AXES, None)),
        out_specs=(P(AXES, None), P(AXES, None), weights),
        check_vma=False,
    )
```

```python
import math

import jax
import jax.numpy as jnp
import numpy as np
from jax import lax
from jax.experimental import pallas as pl
from jax.experimental.pallas import tpu as pltpu
from jax.sharding import Mesh
from jax.sharding import PartitionSpec as P

STEP = 1000

beta_first = 0.9
beta_second = 0.999
adam_epsilon = 1e-08

AXES = ("z_lo", "x", "y", "z_hi", "core")
Z = ("z_hi", "z_lo")
RANK = 512
TOKENS = 65536
KVW = 1024
QUARTER = 2048


def owner_row(core, xy, z):
    x, y = xy >> 2, xy & 3
    z_hi, z_lo = z >> 2, z & 3
    return (((z_lo * 4 + x) * 4 + y) * 4 + z_hi) * 2 + core


def reorder(basis, rows):
    pick = (lax.broadcasted_iota(jnp.int32, (RANK, RANK), 0) == rows[None, :]).astype(jnp.bfloat16)
    return jnp.dot(basis, pick, preferred_element_type=jnp.float32).astype(jnp.bfloat16)


def exchange(blocks, axes):
    return lax.all_to_all(blocks, axes, 0, 0, tiled=True)


def spread(block, axes, count):
    return exchange(jnp.broadcast_to(block[None], (count, *block.shape)), axes)


def pack_kernel(x_ref, tokens_ref, cotangent_ref, *out_refs):
    for k, out_ref in enumerate(out_refs):
        at = (x_ref[0] + k) & 3
        offset = pl.multiple_of((at & 1) * 256 + (at >> 1) * 128, 128)
        for block in range(16):
            out_ref[:, block * 128 : block * 128 + 128] = tokens_ref[
                :, pl.ds(pl.multiple_of(block * 512 + offset, 128), 128)
            ]
        out_ref[:, QUARTER:] = cotangent_ref[...]


def pack(x_at, tokens, cotangent):
    rows = 32
    return pl.pallas_call(
        pack_kernel,
        grid=(128 // rows,),
        in_specs=[
            pl.BlockSpec(memory_space=pltpu.SMEM),
            pl.BlockSpec((rows, 8192), lambda i: (i, 0)),
            pl.BlockSpec((rows, KVW), lambda i: (i, 0)),
        ],
        out_specs=[pl.BlockSpec((rows, QUARTER + KVW), lambda i: (i, 0))] * 4,
        out_shape=[jax.ShapeDtypeStruct((128, QUARTER + KVW), jnp.bfloat16)] * 4,
        compiler_params=pltpu.CompilerParams(vmem_limit_bytes=32 * 2**20),
        cost_estimate=pl.CostEstimate(flops=0, bytes_accessed=6 * 2**20, transcendentals=0),
        name="pack",
    )(x_at[None], tokens, cotangent)


def join_kernel(*refs):
    *pieces, _, out_ref = refs
    for k, piece in enumerate(pieces):
        rows = piece.shape[0]
        out_ref[k * rows : k * rows + rows] = piece[...]


def join(pieces, other):
    rows, columns = pieces[0].shape
    vmem = pl.BlockSpec(memory_space=pltpu.VMEM)
    return pl.pallas_call(
        join_kernel,
        in_specs=[vmem] * len(pieces) + [pl.BlockSpec(memory_space=pl.ANY)],
        out_specs=vmem,
        out_shape=jax.ShapeDtypeStruct((rows * len(pieces), columns), jnp.bfloat16),
        compiler_params=pltpu.CompilerParams(vmem_limit_bytes=16 * 2**20),
        cost_estimate=pl.CostEstimate(flops=0, bytes_accessed=2**20, transcendentals=0),
        name="join",
    )(*pieces, other)


def project_kernel(*refs):
    *pieces, whole_ref, out_ref, split_ref, sum_ref = refs
    whole = whole_ref[...]
    at, tokens = 0, split_ref.shape[0] // 2
    for piece in pieces:
        rows = piece.shape[0]
        reduced = jnp.dot(piece[:, :QUARTER], whole, preferred_element_type=jnp.float32)
        high = reduced.astype(jnp.bfloat16)
        low = (reduced - high.astype(jnp.float32)).astype(jnp.bfloat16)
        split_ref[at : at + rows] = high
        split_ref[tokens + at : tokens + at + rows] = low
        at += rows
    for n in range(0, KVW, 256):
        columns = [piece[:, QUARTER + n : QUARTER + n + 256] for piece in pieces]
        sum_ref[:, n : n + 256] = lax.dot_general(
            split_ref[...],
            jnp.concatenate(columns + columns, axis=0),
            (((0,), (0,)), ((), ())),
            preferred_element_type=jnp.float32,
        )
    top = jnp.max(jnp.abs(sum_ref[...]), axis=1, keepdims=True)
    exponent = jnp.ceil(jnp.log2(jnp.maximum(top, 1e-36))) + 1.0
    exponent = jnp.broadcast_to(exponent, (256, 128))
    scale = jnp.exp2(-exponent)
    out_ref[:, 8] = exponent.reshape(16, 16, 128)
    for n in range(8):
        out_ref[:, n] = (sum_ref[:, n * 128 : n * 128 + 128] * scale).reshape(16, 16, 128)


def project(pieces, whole):
    vmem = pl.BlockSpec(memory_space=pltpu.VMEM)
    return pl.pallas_call(
        project_kernel,
        in_specs=[vmem] * (len(pieces) + 1),
        out_specs=vmem,
        out_shape=jax.ShapeDtypeStruct((16, 9, 16, 128), jnp.float32),
        scratch_shapes=[
            pltpu.VMEM((2048, 256), jnp.bfloat16),
            pltpu.VMEM((256, KVW), jnp.float32),
        ],
        compiler_params=pltpu.CompilerParams(vmem_limit_bytes=40 * 2**20),
        cost_estimate=pl.CostEstimate(
            flops=2 * 2**30, bytes_accessed=8 * 2**20, transcendentals=0
        ),
        name="project",
    )(*pieces, whole)


def decode_kernel(core_ref, basis_ref, own_ref, other_ref, out_ref):
    total = None
    for at, rows_ref in ((core_ref[0], own_ref), (1 - core_ref[0], other_ref)):
        half = basis_ref[:, pl.ds(pl.multiple_of(at * 256, 256), 256)]
        term = jnp.dot(half, rows_ref[...], preferred_element_type=jnp.float32)
        total = term if total is None else total + term
    out_ref[...] = total.astype(jnp.bfloat16)


def decode(core_at, basis, own, other):
    vmem = pl.BlockSpec(memory_space=pltpu.VMEM)
    return pl.pallas_call(
        decode_kernel,
        in_specs=[pl.BlockSpec(memory_space=pltpu.SMEM)] + [vmem] * 3,
        out_specs=vmem,
        out_shape=jax.ShapeDtypeStruct((256, KVW), jnp.bfloat16),
        compiler_params=pltpu.CompilerParams(vmem_limit_bytes=16 * 2**20),
        cost_estimate=pl.CostEstimate(flops=2**28, bytes_accessed=2**21, transcendentals=0),
        name="decode",
    )(core_at[None], basis, own, other)


def adam_kernel(parts_ref, first_hbm, second_hbm, new_first_ref, new_second_ref, normalized_ref,
                first_ref, second_ref, step_ref, semaphores):
    fetches = [
        pltpu.make_async_copy(first_hbm, first_ref, semaphores.at[0]),
        pltpu.make_async_copy(second_hbm, second_ref, semaphores.at[1]),
    ]
    for fetch in fetches:
        fetch.start()
    shares = jnp.sum(parts_ref[...], axis=0) * (1.0 / math.sqrt(TOKENS))
    for fetch in fetches:
        fetch.wait()
    corr_first = 1.0 - beta_first**STEP
    corr_second = 1.0 - beta_second**STEP
    for n in range(8):
        columns = slice(n * 128, n * 128 + 128)
        share = shares[n : n + 1]
        new_first = beta_first * first_ref[:, columns] + (1.0 - beta_first) * share
        new_second = beta_second * second_ref[:, columns] + (1.0 - beta_second) * share * share
        new_first_ref[:, columns] = new_first
        new_second_ref[:, columns] = new_second
        step_ref[n : n + 1] = (
            new_first / corr_first / (jnp.sqrt(new_second / corr_second) + adam_epsilon)
        )
    normalized_ref[...] = step_ref[...].astype(jnp.bfloat16)


def adam(parts, first, second):
    vmem, anywhere = pl.BlockSpec(memory_space=pltpu.VMEM), pl.BlockSpec(memory_space=pl.ANY)
    row = jax.ShapeDtypeStruct((1, KVW), jnp.float32)
    return pl.pallas_call(
        adam_kernel,
        in_specs=[vmem, anywhere, anywhere],
        out_specs=[vmem] * 3,
        out_shape=[row, row, jax.ShapeDtypeStruct((8, 128), jnp.bfloat16)],
        scratch_shapes=[
            pltpu.VMEM((1, KVW), jnp.float32),
            pltpu.VMEM((1, KVW), jnp.float32),
            pltpu.VMEM((8, 128), jnp.float32),
            pltpu.SemaphoreType.DMA((2,)),
        ],
        compiler_params=pltpu.CompilerParams(vmem_limit_bytes=48 * 2**20),
        cost_estimate=pl.CostEstimate(flops=2**14, bytes_accessed=2**16, transcendentals=2**10),
        name="adam",
    )(parts, first, second)


def local(normed_input, value_cotangent, basis, first_moment, second_moment):
    x_at, core_at = (lax.axis_index(a) for a in ("x", "core"))
    swap = [(0, 1), (1, 0)]
    place = np.arange(RANK, dtype=np.int32)
    by_core = owner_row(place >> 8, place >> 4 & 15, place & 15)
    with jax.named_scope("tokens_x"):
        packed = pack(x_at, normed_input, value_cotangent)
        pieces = [packed[0]] + [
            lax.ppermute(packed[k], "x", [(i, (i + k) % 4) for i in range(4)]) for k in (1, 3, 2)
        ]
    def gather(rows):
        with jax.named_scope("gather_core"):
            low, high = rows[:, :256], rows[:, 256:]
            theirs = lax.ppermute(jnp.where(core_at == 0, high, low), "core", swap)
            chunk = jnp.where(core_at == (x_at & 1), jnp.where(core_at == 0, low, high), theirs)
        with jax.named_scope("gather_z"):
            return spread(chunk, "z_hi", 4).reshape(512, 256)

    with jax.named_scope("gather"):
        rows = lax.dynamic_slice_in_dim(basis, (x_at >> 1) * 128, 128, 0)
        rows = reorder(rows, by_core)
        line = lax.cond(
            x_at < 4, gather, lambda rows: jnp.zeros((512, 256), jnp.bfloat16),
            join([rows], packed[1]),
        )
    with jax.named_scope("gather_y"):
        whole = spread(line, "y", 4).reshape(QUARTER, 256)
    with jax.named_scope("tokens_core"):
        held = join(pieces, line)
        held = [held, lax.ppermute(held, "core", swap)]
    with jax.named_scope("project"):
        partial = project(held, whole)
    with jax.named_scope("reduce_xy"):
        parts = exchange(partial.astype(jnp.float16), ("x", "y")).astype(jnp.float32)
        summed = jnp.sum(parts[:, :8] * jnp.exp2(parts[:, 8:]), axis=0).transpose(1, 0, 2)
    with jax.named_scope("reduce_z"):
        parts = exchange(summed, Z)
    with jax.named_scope("adam"):
        new_first, new_second, normalized = adam(parts, first_moment, second_moment)
    with jax.named_scope("spread_z"):
        column = spread(normalized, Z, 16).reshape(16, KVW)
    with jax.named_scope("spread_xy"):
        own = spread(column, ("x", "y"), 16).reshape(256, KVW)
    with jax.named_scope("spread_core"):
        other = lax.ppermute(own, "core", swap)
    with jax.named_scope("decode"):
        update = decode(core_at, reorder(basis, by_core), own, other)
    return new_first, new_second, update


def solution(mesh):
    fine = Mesh(mesh.devices.reshape(4, 4, 4, 4, 2), AXES)
    weights = P(("y", "z_hi", "core"), None)
    return jax.shard_map(
        local,
        mesh=fine,
        in_specs=(P(AXES, None), P(AXES, None), weights, P(AXES, None), P(AXES, None)),
        out_specs=(P(AXES, None), P(AXES, None), weights),
        check_vma=False,
    )
```

```python
import math

import jax
import jax.numpy as jnp
import numpy as np
from jax import lax
from jax.experimental import pallas as pl
from jax.experimental.pallas import tpu as pltpu
from jax.sharding import Mesh
from jax.sharding import PartitionSpec as P

STEP = 1000

beta_first = 0.9
beta_second = 0.999
adam_epsilon = 1e-08

AXES = ("z_lo", "x", "y", "z_hi", "core")
Z = ("z_hi", "z_lo")
RANK = 512
TOKENS = 65536
KVW = 1024
QUARTER = 2048


def owner_row(core, xy, z):
    x, y = xy >> 2, xy & 3
    z_hi, z_lo = z >> 2, z & 3
    return (((z_lo * 4 + x) * 4 + y) * 4 + z_hi) * 2 + core


def reorder(basis, rows):
    pick = (lax.broadcasted_iota(jnp.int32, (RANK, RANK), 0) == rows[None, :]).astype(jnp.bfloat16)
    return jnp.dot(basis, pick, preferred_element_type=jnp.float32).astype(jnp.bfloat16)


def exchange(blocks, axes):
    return lax.all_to_all(blocks, axes, 0, 0, tiled=True)


def spread(block, axes, count):
    return exchange(jnp.broadcast_to(block[None], (count, *block.shape)), axes)


def pack_kernel(x_ref, tokens_ref, cotangent_ref, *out_refs):
    for k, out_ref in enumerate(out_refs):
        at = (x_ref[0] + k) & 3
        offset = pl.multiple_of((at & 1) * 256 + (at >> 1) * 128, 128)
        for block in range(16):
            out_ref[:, block * 128 : block * 128 + 128] = tokens_ref[
                :, pl.ds(pl.multiple_of(block * 512 + offset, 128), 128)
            ]
        out_ref[:, QUARTER:] = cotangent_ref[...]


def pack(x_at, tokens, cotangent):
    rows = 32
    return pl.pallas_call(
        pack_kernel,
        grid=(128 // rows,),
        in_specs=[
            pl.BlockSpec(memory_space=pltpu.SMEM),
            pl.BlockSpec((rows, 8192), lambda i: (i, 0)),
            pl.BlockSpec((rows, KVW), lambda i: (i, 0)),
        ],
        out_specs=[pl.BlockSpec((rows, QUARTER + KVW), lambda i: (i, 0))] * 4,
        out_shape=[jax.ShapeDtypeStruct((128, QUARTER + KVW), jnp.bfloat16)] * 4,
        compiler_params=pltpu.CompilerParams(vmem_limit_bytes=60 * 2**20),
        cost_estimate=pl.CostEstimate(flops=0, bytes_accessed=6 * 2**20, transcendentals=0),
        name="pack",
    )(x_at[None], tokens, cotangent)


def join_kernel(*refs):
    *pieces, _, out_ref = refs
    for k, piece in enumerate(pieces):
        rows = piece.shape[0]
        out_ref[k * rows : k * rows + rows] = piece[...]


def join(pieces, other):
    rows, columns = pieces[0].shape
    vmem = pl.BlockSpec(memory_space=pltpu.VMEM)
    return pl.pallas_call(
        join_kernel,
        in_specs=[vmem] * len(pieces) + [pl.BlockSpec(memory_space=pl.ANY)],
        out_specs=vmem,
        out_shape=jax.ShapeDtypeStruct((rows * len(pieces), columns), jnp.bfloat16),
        compiler_params=pltpu.CompilerParams(vmem_limit_bytes=16 * 2**20),
        cost_estimate=pl.CostEstimate(flops=0, bytes_accessed=2**20, transcendentals=0),
        name="join",
    )(*pieces, other)


def project_kernel(*refs):
    *pieces, whole_ref, out_ref, split_ref, sum_ref = refs
    whole = whole_ref[...]
    at, tokens = 0, split_ref.shape[0] // 2
    for piece in pieces:
        rows = piece.shape[0]
        reduced = jnp.dot(piece[:, :QUARTER], whole, preferred_element_type=jnp.float32)
        high = reduced.astype(jnp.bfloat16)
        low = (reduced - high.astype(jnp.float32)).astype(jnp.bfloat16)
        split_ref[at : at + rows] = high
        split_ref[tokens + at : tokens + at + rows] = low
        at += rows
    for n in range(0, KVW, 256):
        columns = [piece[:, QUARTER + n : QUARTER + n + 256] for piece in pieces]
        sum_ref[:, n : n + 256] = lax.dot_general(
            split_ref[...],
            jnp.concatenate(columns + columns, axis=0),
            (((0,), (0,)), ((), ())),
            preferred_element_type=jnp.float32,
        )
    top = jnp.max(jnp.abs(sum_ref[...]), axis=1, keepdims=True)
    exponent = jnp.ceil(jnp.log2(jnp.maximum(top, 1e-36))) + 1.0
    exponent = jnp.broadcast_to(exponent, (256, 128))
    scale = jnp.exp2(-exponent)
    out_ref[:, 8] = exponent.reshape(16, 16, 128)
    for n in range(8):
        out_ref[:, n] = (sum_ref[:, n * 128 : n * 128 + 128] * scale).reshape(16, 16, 128)


def project(pieces, whole):
    vmem = pl.BlockSpec(memory_space=pltpu.VMEM)
    return pl.pallas_call(
        project_kernel,
        in_specs=[vmem] * (len(pieces) + 1),
        out_specs=vmem,
        out_shape=jax.ShapeDtypeStruct((16, 9, 16, 128), jnp.float32),
        scratch_shapes=[
            pltpu.VMEM((2048, 256), jnp.bfloat16),
            pltpu.VMEM((256, KVW), jnp.float32),
        ],
        compiler_params=pltpu.CompilerParams(vmem_limit_bytes=40 * 2**20),
        cost_estimate=pl.CostEstimate(
            flops=2 * 2**30, bytes_accessed=8 * 2**20, transcendentals=0
        ),
        name="project",
    )(*pieces, whole)


def decode_kernel(core_ref, basis_ref, own_ref, other_ref, out_ref):
    total = None
    for at, rows_ref in ((core_ref[0], own_ref), (1 - core_ref[0], other_ref)):
        half = basis_ref[:, pl.ds(pl.multiple_of(at * 256, 256), 256)]
        term = jnp.dot(half, rows_ref[...], preferred_element_type=jnp.float32)
        total = term if total is None else total + term
    out_ref[...] = total.astype(jnp.bfloat16)


def decode(core_at, basis, own, other):
    vmem = pl.BlockSpec(memory_space=pltpu.VMEM)
    return pl.pallas_call(
        decode_kernel,
        in_specs=[pl.BlockSpec(memory_space=pltpu.SMEM)] + [vmem] * 3,
        out_specs=vmem,
        out_shape=jax.ShapeDtypeStruct((256, KVW), jnp.bfloat16),
        compiler_params=pltpu.CompilerParams(vmem_limit_bytes=16 * 2**20),
        cost_estimate=pl.CostEstimate(flops=2**28, bytes_accessed=2**21, transcendentals=0),
        name="decode",
    )(core_at[None], basis, own, other)


def adam_kernel(parts_ref, first_hbm, second_hbm, new_first_ref, new_second_ref, normalized_ref,
                first_ref, second_ref, step_ref, semaphores):
    fetches = [
        pltpu.make_async_copy(first_hbm, first_ref, semaphores.at[0]),
        pltpu.make_async_copy(second_hbm, second_ref, semaphores.at[1]),
    ]
    for fetch in fetches:
        fetch.start()
    shares = jnp.sum(parts_ref[...], axis=0) * (1.0 / math.sqrt(TOKENS))
    for fetch in fetches:
        fetch.wait()
    corr_first = 1.0 - beta_first**STEP
    corr_second = 1.0 - beta_second**STEP
    for n in range(8):
        columns = slice(n * 128, n * 128 + 128)
        share = shares[n : n + 1]
        new_first = beta_first * first_ref[:, columns] + (1.0 - beta_first) * share
        new_second = beta_second * second_ref[:, columns] + (1.0 - beta_second) * share * share
        new_first_ref[:, columns] = new_first
        new_second_ref[:, columns] = new_second
        step_ref[n : n + 1] = (
            new_first / corr_first / (jnp.sqrt(new_second / corr_second) + adam_epsilon)
        )
    normalized_ref[...] = step_ref[...].astype(jnp.bfloat16)


def adam(parts, first, second):
    vmem, anywhere = pl.BlockSpec(memory_space=pltpu.VMEM), pl.BlockSpec(memory_space=pl.ANY)
    row = jax.ShapeDtypeStruct((1, KVW), jnp.float32)
    return pl.pallas_call(
        adam_kernel,
        in_specs=[vmem, anywhere, anywhere],
        out_specs=[vmem] * 3,
        out_shape=[row, row, jax.ShapeDtypeStruct((8, 128), jnp.bfloat16)],
        scratch_shapes=[
            pltpu.VMEM((1, KVW), jnp.float32),
            pltpu.VMEM((1, KVW), jnp.float32),
            pltpu.VMEM((8, 128), jnp.float32),
            pltpu.SemaphoreType.DMA((2,)),
        ],
        compiler_params=pltpu.CompilerParams(vmem_limit_bytes=48 * 2**20),
        cost_estimate=pl.CostEstimate(flops=2**14, bytes_accessed=2**16, transcendentals=2**10),
        name="adam",
    )(parts, first, second)


def local(normed_input, value_cotangent, basis, first_moment, second_moment):
    x_at, z_lo_at, core_at = (lax.axis_index(a) for a in ("x", "z_lo", "core"))
    swap = [(0, 1), (1, 0)]
    place = np.arange(RANK, dtype=np.int32)
    by_core = owner_row(place >> 8, place >> 4 & 15, place & 15)
    with jax.named_scope("tokens_x"):
        packed = pack(x_at, normed_input, value_cotangent)
        pieces = [packed[0]] + [
            lax.ppermute(packed[k], "x", [(i, (i + k) % 4) for i in range(4)]) for k in (1, 3, 2)
        ]
    with jax.named_scope("gather_core"):
        rows = lax.dynamic_slice_in_dim(basis, (x_at >> 1) * 128 + z_lo_at * 32, 32, 0)
        rows = reorder(rows, by_core)
        low, high = rows[:, :256], rows[:, 256:]
        theirs = lax.ppermute(jnp.where(core_at == 0, high, low), "core", swap)
        chunk = jnp.where(core_at == (x_at & 1), jnp.where(core_at == 0, low, high), theirs)

    def gather(chunk):
        with jax.named_scope("gather_z"):
            return spread(chunk, Z, 16).reshape(512, 256)

    with jax.named_scope("gather"):
        line = lax.cond(
            x_at < 4, gather, lambda chunk: jnp.zeros((512, 256), jnp.bfloat16), chunk
        )
    with jax.named_scope("gather_y"):
        whole = spread(line, "y", 4).reshape(QUARTER, 256)
    with jax.named_scope("tokens_core"):
        held = join(pieces, line)
        held = [held, lax.ppermute(held, "core", swap)]
    with jax.named_scope("project"):
        partial = project(held, whole)
    with jax.named_scope("reduce_xy"):
        parts = exchange(partial.astype(jnp.float16), ("x", "y")).astype(jnp.float32)
        summed = jnp.sum(parts[:, :8] * jnp.exp2(parts[:, 8:]), axis=0).transpose(1, 0, 2)
    with jax.named_scope("reduce_z"):
        parts = exchange(summed, Z)
    with jax.named_scope("adam"):
        new_first, new_second, normalized = adam(parts, first_moment, second_moment)
    with jax.named_scope("spread_z"):
        column = spread(normalized, Z, 16).reshape(16, KVW)
    with jax.named_scope("spread_xy"):
        own = spread(column, ("x", "y"), 16).reshape(256, KVW)
    with jax.named_scope("spread_core"):
        other = lax.ppermute(own, "core", swap)
    with jax.named_scope("decode"):
        update = decode(core_at, reorder(basis, by_core), own, other)
    return new_first, new_second, update


def solution(mesh):
    fine = Mesh(mesh.devices.reshape(4, 4, 4, 4, 2), AXES)
    weights = P(("y", "z_hi", "core"), None)
    return jax.shard_map(
        local,
        mesh=fine,
        in_specs=(P(AXES, None), P(AXES, None), weights, P(AXES, None), P(AXES, None)),
        out_specs=(P(AXES, None), P(AXES, None), weights),
        check_vma=False,
    )
```
